32 devices in a mesh: seq: 8 (over z, x), tp: 4 (over y, core).
Axes of the slice: x: 2, y: 2, z: 4, core: 2. Of those that a mesh axis runs over, the one named last changes fastest.
Arguments:
- tokens: bfloat16 [4, 16, 5120], P(None, None, 'seq'), may hold values from -32 to 32
- attn_gain: bfloat16 [5120], P('seq'), may hold values from 0.099609375 to 1.8984375
- w_query: bfloat16 [5120, 4096], P('seq', 'tp'), may hold values from -0.078125 to 0.078125
- w_key: bfloat16 [5120, 1024], P('seq', 'tp'), may hold values from -0.078125 to 0.078125
- w_value: bfloat16 [5120, 1024], P('seq', 'tp'), may hold values from -0.078125 to 0.078125
- w_out: bfloat16 [4096, 5120], P('tp', 'seq'), may hold values from -0.09375 to 0.09375
- ffn_gain: bfloat16 [5120], replicated, may hold values from 0.099609375 to 1.8984375
- w_gate: bfloat16 [5120, 32768], P(None, ('seq', 'tp')), may hold values from -0.078125 to 0.078125
- w_up: bfloat16 [5120, 32768], P(None, ('seq', 'tp')), may hold values from -0.078125 to 0.078125
- w_down: bfloat16 [32768, 5120], P(('seq', 'tp')), may hold values from -0.0625 to 0.0625
- key_cache: bfloat16 [16, 1024, 8, 128], P(None, 'seq', 'tp'), may hold values from -96 to 96
- value_cache: bfloat16 [16, 1024, 8, 128], P(None, 'seq', 'tp'), may hold values from -48 to 48
- lengths: int32 [16], replicated, may hold values from 1 to 1020, as said below
Outputs:
- hidden_out: bfloat16 [4, 16, 5120], P(None, None, 'seq')
- keys_out: bfloat16 [16, 1024, 8, 128], P(None, 'seq', 'tp')
- values_out: bfloat16 [16, 1024, 8, 128], P(None, 'seq', 'tp')
The draws below stay inside these ranges and needn't reach their ends.
Inputs may be any that keep to these rules, and one draw needn't show every extreme that they name: `lengths`: some request's length is exactly 1020.
All inputs are finite; a program needn't handle non-finite values.
Results may differ from the reference program's by a relative error of at most 0.012.
The reference program's roundings to bfloat16 on the way count: a program that leaves them out, or rounds other values in their place, can miss the bound.
Values may be sent and summed in bfloat16 or wider, within the bound.
No kernel may reach another device: no remote copies, remote signals or barrier semaphores. Data moves between devices by JAX's collectives and lax.ppermute only.
A program may use at most 128 MiB of HBM per device.

```python
import math
import jax
import jax.numpy as jnp
from jax import lax

D = 5120
HEADS = 32
KVH = 8
HD = 128
FF = 32768
REQ = 16
STEPS = 4
SEQ_LEN = 1024


def draw_tokens(key, part):
    ramp = jnp.arange(D, dtype=jnp.float32) / D
    rise = jnp.exp(ramp * jnp.log(4.0))
    norm = jnp.sqrt(jnp.mean(rise * rise))
    base = jnp.clip(jax.random.normal(key, (STEPS, REQ, D), jnp.float32), -6.0, 6.0)
    values = base * (rise / norm)[None, None, :]
    return jnp.clip(values, -32.0, 32.0).astype(jnp.bfloat16)


def draw_lengths(key, part):
    longest = SEQ_LEN - STEPS
    drawn = jax.random.randint(jax.random.fold_in(key, 101), (REQ,), 1, longest + 1)
    chosen = jax.random.randint(jax.random.fold_in(key, 103), (), 0, REQ)
    return jnp.where(jnp.arange(REQ) == chosen, longest, drawn).astype(jnp.int32)


def stale_slots(key):
    lengths = draw_lengths(key, 0)
    places = jnp.arange(SEQ_LEN, dtype=jnp.int32)[None, :]
    return (places >= lengths[:, None]) & (places < lengths[:, None] + STEPS)


def stale_entries(key, low, high):
    magnitude = jax.random.uniform(jax.random.fold_in(key, 1), (REQ, SEQ_LEN, KVH, HD), jnp.float32, low, high)
    upward = jax.random.bernoulli(jax.random.fold_in(key, 2), 0.5, (REQ, SEQ_LEN, KVH, HD))
    return jnp.where(upward, magnitude, -magnitude)


def draw_key_cache(key, part):
    base = jax.random.normal(jax.random.fold_in(key, 201), (REQ, SEQ_LEN, KVH, HD), jnp.float32)
    scale = 2.5
    fresh = jnp.clip(base * scale, -96.0, 96.0)
    stale = stale_entries(jax.random.fold_in(key, 211), 48.0, 96.0)
    chosen = stale_slots(key)[:, :, None, None]
    return jnp.where(chosen, stale, fresh).astype(jnp.bfloat16)


def draw_value_cache(key, part):
    fresh = jnp.clip(jax.random.normal(jax.random.fold_in(key, 301), (REQ, SEQ_LEN, KVH, HD), jnp.float32), -6.0, 6.0)
    stale = stale_entries(jax.random.fold_in(key, 311), 24.0, 48.0)
    chosen = stale_slots(key)[:, :, None, None]
    return jnp.where(chosen, stale, fresh).astype(jnp.bfloat16)


def with_spikes(values, key, source, target, shards_of, factor):
    owner, partner = [(jnp.arange(values.shape[dim]) // (values.shape[dim] // shards_of)).reshape([-1 if axis == dim else 1 for axis in range(values.ndim)]) for dim in (source, target)]
    chosen = jax.random.permutation(key, shards_of)[partner]
    strong = (owner == chosen) | (owner == (partner + shards_of // 2) % shards_of)
    return jnp.where(strong, factor * values, values)


def block_levels(rng, dims, cuts, smallest, largest):
    def one(dim, blocks):
        steps = jax.random.uniform(jax.random.fold_in(jax.random.fold_in(rng, 6), dim), (blocks,), jnp.float32, smallest / len(cuts), largest / len(cuts))
        return jnp.repeat(jnp.exp(steps), dims[dim] // blocks).reshape((-1,) + (1,) * (len(dims) - dim - 1))

    gain = one(*cuts[0])
    for cut in cuts[1:]:
        gain = gain * one(*cut)
    return gain


def bell_draw(rng, shape, width, bound, split=(), held_as=jnp.bfloat16):
    array = width * jax.random.normal(rng, shape, jnp.float32)
    if split:
        array = array * block_levels(rng, shape, split, -0.22, 0.18)
    return jnp.clip(array, -bound, bound).astype(held_as)


def gaussian_with(own_key, extent, spread, bound, pieces, heavy, kind=jnp.bfloat16):
    array = spread * jax.random.normal(own_key, extent, jnp.float32)
    if pieces:
        array = array * block_levels(own_key, extent, pieces, -0.22, 0.18)
    return jnp.clip(with_spikes(array, jax.random.fold_in(own_key, 3), *heavy), -bound, bound).astype(kind)


def setup_inputs(seed: int = 0) -> dict:
    seeds = jax.random.split(jax.random.key(seed), 14)
    return {
        "tokens": draw_tokens(jax.random.fold_in(seeds[13], 71), 0),
        "attn_gain": jnp.clip(1.0 + 0.18 * jax.random.normal(seeds[1], (D,), jnp.float32), 0.099609375, 1.8984375).astype(jnp.bfloat16),
        "w_query": bell_draw(seeds[2], (D, HEADS * HD), D ** -0.5, 0.078125, ((0, 8), (1, 4))),
        "w_key": bell_draw(seeds[3], (D, KVH * HD), D ** -0.5, 0.078125, ((0, 8), (1, 4))),
        "w_value": bell_draw(seeds[4], (D, KVH * HD), D ** -0.5, 0.078125, ((0, 8), (1, 4))),
        "w_out": bell_draw(seeds[5], (HEADS * HD, D), (HEADS * HD) ** -0.5, 0.09375, ((0, 4), (1, 8))),
        "ffn_gain": jnp.clip(1.0 + 0.18 * jax.random.normal(seeds[6], (D,), jnp.float32), 0.099609375, 1.8984375).astype(jnp.bfloat16),
        "w_gate": bell_draw(seeds[7], (D, FF), D ** -0.5, 0.078125, ((1, 32),)),
        "w_up": bell_draw(seeds[8], (D, FF), D ** -0.5, 0.078125, ((1, 32),)),
        "w_down": gaussian_with(seeds[9], (FF, D), FF ** -0.5, 0.0625, ((0, 32),), (0, 1, 32, 2.75)),
        "key_cache": draw_key_cache(jax.random.fold_in(seeds[13], 71), 0),
        "value_cache": draw_value_cache(jax.random.fold_in(seeds[13], 71), 0),
        "lengths": draw_lengths(jax.random.fold_in(seeds[13], 71), 0),
    }


def rotate(vectors, position):
    half = vectors.shape[-1] // 2
    freqs = jnp.exp(jnp.arange(half, dtype=jnp.float32) * (-2.0 * math.log(100000000.0) / vectors.shape[-1]))
    angles = position.astype(jnp.float32)[:, None] * freqs[None, :]
    cosine = jnp.cos(angles)[:, None, :]
    sine = jnp.sin(angles)[:, None, :]
    first = vectors[..., :half]
    second = vectors[..., half:]
    return jnp.concatenate([first * cosine - second * sine, second * cosine + first * sine], axis=-1)

def one_request(packed):
    query, keys, values, position = packed
    grouped = query.astype(jnp.float32).reshape(KVH, HEADS // KVH, HD)
    scores = jnp.einsum('gjd,pgd->gjp', grouped, keys.astype(jnp.float32)) * HD ** (-0.5)
    live = (jnp.arange(SEQ_LEN) <= position)[None, None, :]
    masked = jnp.where(live, scores, -1e+30)
    top = lax.optimization_barrier(jnp.max(masked, axis=-1))
    expo = jnp.where(live, jnp.exp(masked - top[..., None]), 0.0)
    denom = lax.optimization_barrier(jnp.sum(expo, axis=-1))
    weights = expo.astype(jnp.bfloat16)
    summed = jnp.einsum('gjp,pgd->gjd', weights.astype(jnp.float32), values.astype(jnp.float32))
    return (summed / denom[..., None]).reshape(HEADS, HD).astype(jnp.bfloat16)

def reference(tokens, attn_gain, w_query, w_key, w_value, w_out, ffn_gain, w_gate, w_up, w_down, key_cache, value_cache, lengths):
    req_index = jnp.arange(REQ)
    results = []
    for step in range(STEPS):
        residual = tokens[step].astype(jnp.float32)
        scale_in = lax.rsqrt(lax.optimization_barrier(jnp.mean(residual * residual, axis=1, keepdims=True)) + 1e-05)
        normed = (residual * attn_gain.astype(jnp.float32)).astype(jnp.bfloat16)
        query = jnp.dot(normed, w_query, preferred_element_type=jnp.float32) * scale_in
        key_new = jnp.dot(normed, w_key, preferred_element_type=jnp.float32) * scale_in
        value_new = jnp.dot(normed, w_value, preferred_element_type=jnp.float32) * scale_in
        position = (lengths + step).astype(jnp.int32)
        query = rotate(query.reshape(REQ, HEADS, HD), position).astype(jnp.bfloat16)
        key_new = rotate(key_new.reshape(REQ, KVH, HD), position).astype(jnp.bfloat16)
        value_new = value_new.reshape(REQ, KVH, HD).astype(jnp.bfloat16)
        key_cache = key_cache.at[req_index, position].set(key_new)
        value_cache = value_cache.at[req_index, position].set(value_new)
        attended = lax.map(one_request, (query, key_cache, value_cache, position))
        mixed = residual + jnp.dot(attended.reshape(REQ, HEADS * HD), w_out, preferred_element_type=jnp.float32)
        scale_mid = lax.rsqrt(lax.optimization_barrier(jnp.mean(mixed * mixed, axis=1, keepdims=True)) + 1e-05)
        ffn_in = (mixed * ffn_gain.astype(jnp.float32)).astype(jnp.bfloat16)
        gate_raw = jnp.dot(ffn_in, w_gate, preferred_element_type=jnp.float32) * scale_mid
        up_raw = jnp.dot(ffn_in, w_up, preferred_element_type=jnp.float32) * scale_mid
        hidden = (jax.nn.silu(gate_raw) * up_raw).astype(jnp.bfloat16)
        output = mixed + jnp.dot(hidden, w_down, preferred_element_type=jnp.float32)
        results.append(output.astype(jnp.bfloat16))
    return (jnp.stack(results), key_cache, value_cache)
```

```python
import functools
import math

import jax
import jax.numpy as jnp
from jax import lax
from jax.experimental import pallas as pl
from jax.experimental.pallas import tpu as pltpu
from jax.sharding import PartitionSpec as P

F32 = jnp.float32
BF16 = jnp.bfloat16
LANES = 128
VMEM = pl.BlockSpec(memory_space=pltpu.VMEM)
SMEM = pl.BlockSpec(memory_space=pltpu.SMEM)


def call(body, outs, ins, scratch=(), limit=16):
    return pl.pallas_call(
        body,
        out_shape=outs,
        in_specs=ins,
        out_specs=[VMEM] * len(outs),
        scratch_shapes=list(scratch),
        compiler_params=pltpu.CompilerParams(vmem_limit_bytes=limit << 20),
    )


def sds(shape, dtype):
    return jax.ShapeDtypeStruct(shape, dtype)


def lane_ids(rows):
    return lax.broadcasted_iota(jnp.int32, (rows, LANES), 1)


def split3(value):
    high = value.astype(BF16)
    rest = value - high.astype(F32)
    mid = rest.astype(BF16)
    low = (rest - mid.astype(F32)).astype(BF16)
    return high, mid, low


def pack_stats(stats):
    high, mid, low = (part.astype(F32) for part in split3(stats))
    return (high + pltpu.roll(mid, 8, 1) + pltpu.roll(low, 16, 1)).astype(BF16)


def unpack_stats(packed):
    packed = packed.astype(F32)
    return (packed + pltpu.roll(packed, LANES - 8, 1)) + pltpu.roll(packed, LANES - 16, 1)


def project_kernel(x_ref, gain_ref, wq_ref, wk_ref, wv_ref, acc_ref, msg_ref):
    x = x_ref[...].astype(F32)
    normed = (x * gain_ref[...].astype(F32)).astype(BF16)
    squares = jnp.sum(x * x, axis=1, keepdims=True)
    at = 0
    for w_ref in (wq_ref, wk_ref, wv_ref):
        width = w_ref.shape[1]
        part = jnp.dot(normed, w_ref[...], preferred_element_type=F32)
        acc_ref[:, at : at + width] = part
        msg_ref[:, at : at + width] = part.astype(BF16)
        at += width
    stats = jnp.where(lane_ids(x.shape[0]) == 0, squares, 0.0)
    acc_ref[:, at:] = stats
    msg_ref[:, at:] = pack_stats(stats)


def add_kernel(acc_ref, recv_ref, out_ref, msg_ref):
    at = acc_ref.shape[1] - LANES
    total = acc_ref[:, :at] + recv_ref[:, :at].astype(F32)
    out_ref[:, :at] = total
    msg_ref[:, :at] = total.astype(BF16)
    stats = acc_ref[:, at:] + unpack_stats(recv_ref[:, at:])
    stats = jnp.where(lane_ids(stats.shape[0]) == 0, stats, 0.0)
    out_ref[:, at:] = stats
    msg_ref[:, at:] = pack_stats(stats)


def attend_kernel(
    heads,
    kv,
    steps,
    features,
    slot_ref,
    len_ref,
    acc_ref,
    recv_ref,
    cos_ref,
    sin_ref,
    k_ref,
    v_ref,
    k_out,
    v_out,
    o_ref,
    st_ref,
    msg_ref,
    q_buf,
    kn_buf,
    vn_buf,
    o_buf,
    m_buf,
    l_buf,
):
    requests, rows_kv, hd = k_ref.shape
    rows = requests * steps
    group = heads // kv
    block = steps * heads
    fresh = steps * kv
    at = (heads + 2 * kv) * hd
    squares = acc_ref[:, at:] + unpack_stats(recv_ref[:, at:])
    scale = lax.rsqrt(squares[:, 0:1] / features + 1e-05)

    def vector(index):
        cols = slice(index * hd, (index + 1) * hd)
        return (acc_ref[:, cols] + recv_ref[:, cols].astype(F32)) * scale

    def rotated(value):
        return value * cos_ref[...] + pltpu.roll(value, hd // 2, 1) * sin_ref[...]

    def spread(buf, value, index, per_step):
        for t in range(steps):
            buf[pl.ds(t * per_step + index, requests, stride=steps * per_step), :] = value[
                t * requests : (t + 1) * requests
            ]

    for h in range(heads):
        spread(q_buf, rotated(vector(h)), h, heads)
    for g in range(kv):
        spread(kn_buf, rotated(vector(heads + g)), g, kv)
        spread(vn_buf, vector(heads + kv + g), g, kv)

    row = lax.broadcasted_iota(jnp.int32, (block, rows_kv), 0)
    col = lax.broadcasted_iota(jnp.int32, (block, rows_kv), 1)
    same = (row % heads) // group == col % kv
    need = jnp.where(same, col // kv - row // heads, 1 << 29)
    place = lax.broadcasted_iota(jnp.int32, (rows_kv, fresh), 0) - lax.broadcasted_iota(
        jnp.int32, (rows_kv, fresh), 1
    )
    line = lax.broadcasted_iota(jnp.int32, (rows_kv, hd), 0)
    first = slot_ref[0]
    for r in range(requests):
        start = len_ref[r] - first
        base = start * kv
        pick = jnp.where(place == base, 1.0, 0.0).astype(BF16)
        new = (line >= base) & (line < base + fresh)

        def renewed(cache_ref, buf):
            news = buf[r * fresh : (r + 1) * fresh, :].astype(BF16)
            put = jnp.dot(pick, news, preferred_element_type=F32)
            return jnp.where(new, put, cache_ref[r].astype(F32)).astype(BF16)

        keys = renewed(k_ref, kn_buf)
        values = renewed(v_ref, vn_buf)
        k_out[r] = keys
        v_out[r] = values
        query = q_buf[r * block : (r + 1) * block, :].astype(BF16)
        scores = lax.dot_general(
            query, keys, (((1,), (1,)), ((), ())), preferred_element_type=F32
        ) * hd ** (-0.5)
        live = need <= start
        masked = jnp.where(live, scores, -1e30)
        top = jnp.max(masked, axis=1, keepdims=True)
        expo = jnp.where(live, jnp.exp(masked - top), 0.0)
        total = jnp.sum(expo, axis=1, keepdims=True)
        o_buf[r * block : (r + 1) * block, :] = jnp.dot(
            expo.astype(BF16), values, preferred_element_type=F32
        )
        m_buf[r * block : (r + 1) * block, :] = jnp.broadcast_to(top, (block, hd))
        l_buf[r * block : (r + 1) * block, :] = jnp.broadcast_to(total, (block, hd))

    lane = lane_ids(requests)
    for t in range(steps):
        mine = slice(t * requests, (t + 1) * requests)
        stats = jnp.zeros((requests, LANES), F32)
        for h in range(heads):
            take = pl.ds(t * heads + h, requests, stride=block)
            value = o_buf[take, :]
            o_ref[mine, h * hd : (h + 1) * hd] = value
            msg_ref[mine, h * hd : (h + 1) * hd] = value.astype(BF16)
            stats = jnp.where(lane == h, m_buf[take, :], stats)
            stats = jnp.where(lane == 24 + h, l_buf[take, :], stats)
        st_ref[mine, :] = stats
        msg_ref[mine, heads * hd :] = pack_stats(stats)


def merged(heads, o_ref, st_ref, recv_ref):
    hd = o_ref.shape[1] // heads
    mine = st_ref[...]
    theirs = unpack_stats(recv_ref[:, heads * hd :])
    top = jnp.maximum(mine, theirs)
    keep, take = jnp.exp(mine - top), jnp.exp(theirs - top)
    total = mine * pltpu.roll(keep, 24, 1) + theirs * pltpu.roll(take, 24, 1)
    lane = lane_ids(mine.shape[0])
    stats = jnp.where(lane < heads, top, jnp.where((lane >= 24) & (lane < 24 + heads), total, 0.0))

    def head(h):
        cols = slice(h * hd, (h + 1) * hd)
        return o_ref[:, cols] * keep[:, h : h + 1] + recv_ref[:, cols].astype(F32) * take[:, h : h + 1]

    return stats, head


def merge_kernel(heads, o_ref, st_ref, recv_ref, o_out, st_out, msg_out):
    stats, head = merged(heads, o_ref, st_ref, recv_ref)
    hd = o_ref.shape[1] // heads
    for h in range(heads):
        value = head(h)
        o_out[:, h * hd : (h + 1) * hd] = value
        msg_out[:, h * hd : (h + 1) * hd] = value.astype(BF16)
    st_out[...] = stats
    msg_out[:, heads * hd :] = pack_stats(stats)


def finish_kernel(heads, core_ref, o_ref, st_ref, recv_ref, w_ref, mine_ref, other_ref, att_buf):
    stats, head = merged(heads, o_ref, st_ref, recv_ref)
    hd = o_ref.shape[1] // heads
    for h in range(heads):
        att_buf[:, h * hd : (h + 1) * hd] = (head(h) / stats[:, 24 + h : 25 + h]).astype(BF16)
    part = jnp.dot(att_buf[...], w_ref[...], preferred_element_type=F32)
    half = part.shape[0] // 2
    low = core_ref[0] == 0
    mine_ref[...] = jnp.where(low, part[:half], part[half:])
    other_ref[...] = jnp.where(low, part[half:], part[:half])


def hidden_kernel(masks, features, seq_ref, own_ref, far_ref, wg_ref, wu_ref, h_ref):
    count, half, width = own_ref.shape
    width -= LANES
    seq = seq_ref[0]
    squares = []
    for ref in (own_ref, far_ref):
        total = jnp.zeros((half, LANES), F32)
        for j in range(count):
            total += unpack_stats(ref[j, :, :LANES])
        squares.append(total)
    scale = lax.rsqrt(jnp.concatenate(squares, axis=0)[:, 0:1] / features + 1e-05)
    gate = jnp.zeros((2 * half, wg_ref.shape[1]), F32)
    up = jnp.zeros((2 * half, wu_ref.shape[1]), F32)
    for j, mask in enumerate(masks):
        rows = pl.ds(pl.multiple_of((seq ^ mask) * width, 16), width)
        x = jnp.concatenate([own_ref[j, :, LANES:], far_ref[j, :, LANES:]], axis=0)
        gate += jnp.dot(x, wg_ref[rows, :], preferred_element_type=F32)
        up += jnp.dot(x, wu_ref[rows, :], preferred_element_type=F32)
    gate = gate * scale
    up = up * scale
    h_ref[...] = (gate / (1.0 + jnp.exp(-gate)) * up).astype(BF16)


def down_kernel(masks, width, seq_ref, h_ref, w_ref, own_ref, far_ref):
    seq = seq_ref[0]
    half = h_ref.shape[0] // 2
    hidden = h_ref[...]
    for j, mask in enumerate(masks):
        cols = pl.ds(pl.multiple_of((seq ^ mask) * width, LANES), width)
        part = jnp.dot(hidden, w_ref[:, cols], preferred_element_type=F32)
        own_ref[j] = part[:half]
        far_ref[j] = part[half:].astype(BF16)


def per_device(
    n_seq,
    n_tp,
    tokens,
    attn_gain,
    w_query,
    w_key,
    w_value,
    w_out,
    ffn_gain,
    w_gate,
    w_up,
    w_down,
    key_cache,
    value_cache,
    lengths,
):
    steps, requests, width = tokens.shape
    span, kv, hd = key_cache.shape[1:]
    heads = w_query.shape[1] // hd
    rows = steps * requests
    half = rows // 2
    features = width * n_seq
    wide = w_query.shape[1] + w_key.shape[1] + w_value.shape[1] + LANES
    seq = lax.axis_index("seq")
    tp = lax.axis_index("tp")
    seq_bits = [1 << b for b in range(n_seq.bit_length() - 1)]
    masks = [0]
    for bit in reversed(seq_bits):
        masks = masks + [m ^ bit for m in masks]

    def hop(value, axis, bit):
        size = n_seq if axis == "seq" else n_tp
        return lax.ppermute(value, axis, [(i, i ^ bit) for i in range(size)])

    x = tokens.reshape(rows, width)
    core = (tp & 1).astype(jnp.int32)
    seq_arr = seq.astype(jnp.int32).reshape(1)
    core_arr = core.reshape(1)

    positions = (lengths[None, :] + jnp.arange(steps, dtype=jnp.int32)[:, None]).reshape(rows)
    freqs = jnp.exp(jnp.arange(hd // 2, dtype=F32) * (-2.0 * math.log(100000000.0) / hd))
    angles = positions.astype(F32)[:, None] * freqs[None, :]
    cosine, sine = jnp.cos(angles), jnp.sin(angles)
    cosine = jnp.concatenate([cosine, cosine], axis=1)
    sine = jnp.concatenate([-sine, sine], axis=1)

    with jax.named_scope("project"):
        acc, msg = call(
            project_kernel, [sds((rows, wide), F32), sds((rows, wide), BF16)], [VMEM] * 5
        )(x, attn_gain.reshape(1, width), w_query, w_key, w_value)
        for bit in seq_bits[:-1]:
            acc, msg = call(
                add_kernel, [sds((rows, wide), F32), sds((rows, wide), BF16)], [VMEM] * 2
            )(acc, hop(msg, "seq", bit))
        recv = hop(msg, "seq", seq_bits[-1])

    with jax.named_scope("attend"):
        rows_kv = span * kv
        flat = (requests, rows_kv, hd)
        block = steps * heads
        joint = [
            sds((rows, heads * hd), F32),
            sds((rows, LANES), F32),
            sds((rows, heads * hd + LANES), BF16),
        ]
        keys, values, o, st, msg = call(
            functools.partial(attend_kernel, heads, kv, steps, features),
            [sds(flat, BF16), sds(flat, BF16)] + joint,
            [SMEM, SMEM] + [VMEM] * 6,
            [
                pltpu.VMEM((requests * block, hd), F32),
                pltpu.VMEM((requests * steps * kv, hd), F32),
                pltpu.VMEM((requests * steps * kv, hd), F32),
                pltpu.VMEM((requests * block, hd), F32),
                pltpu.VMEM((requests * block, hd), F32),
                pltpu.VMEM((requests * block, hd), F32),
            ],
        )(
            seq_arr * span,
            lengths,
            acc,
            recv,
            cosine,
            sine,
            key_cache.reshape(flat),
            value_cache.reshape(flat),
        )
        for bit in seq_bits[:-1]:
            o, st, msg = call(functools.partial(merge_kernel, heads), joint, [VMEM] * 3)(
                o, st, hop(msg, "seq", bit)
            )
        recv = hop(msg, "seq", seq_bits[-1])

    with jax.named_scope("mix"):
        mine, other = call(
            functools.partial(finish_kernel, heads),
            [sds((half, width), F32)] * 2,
            [SMEM] + [VMEM] * 4,
            [pltpu.VMEM((rows, heads * hd), BF16)],
        )(core_arr, o, st, recv, w_out)
        part = mine + hop(other, "tp", 1)
        for bit in [1 << b for b in range(1, n_tp.bit_length() - 1)]:
            sent = lax.reduce_precision(part, 8, 7)
            part = sent + hop(sent.astype(BF16), "tp", bit).astype(F32)
        own_x = lax.dynamic_slice_in_dim(x, core * half, half, 0).astype(F32)
        mixed = own_x + part
        gain = lax.dynamic_slice_in_dim(ffn_gain, seq * width, width, 0).astype(F32)
        ffn_in = (mixed * gain).astype(BF16)
        squares = jnp.sum(mixed * mixed, axis=1, keepdims=True)
        high = lax.reduce_precision(squares, 8, 7)
        mid = lax.reduce_precision(squares - high, 8, 7)
        low = squares - high - mid
        lane = lane_ids(half)
        stats = jnp.where(lane == 0, high, jnp.where(lane == 8, mid, jnp.where(lane == 16, low, 0.0)))
        pieces = jnp.concatenate([stats.astype(BF16), ffn_in], axis=1)[None]
        for bit in reversed(seq_bits):
            pieces = jnp.concatenate([pieces, hop(pieces, "seq", bit)], axis=0)
        far = hop(pieces, "tp", 1)

    with jax.named_scope("ffn"):
        (hidden,) = call(
            functools.partial(hidden_kernel, masks, features),
            [sds((rows, w_gate.shape[1]), BF16)],
            [SMEM] + [VMEM] * 4,
        )(seq_arr, pieces, far, w_gate, w_up)
        shape = (n_seq, half, width)
        if width % LANES == 0:
            own, far = call(
                functools.partial(down_kernel, masks, width),
                [sds(shape, F32), sds(shape, BF16)],
                [SMEM] + [VMEM] * 2,
            )(seq_arr, hidden, w_down)
        else:
            whole = jnp.dot(hidden, w_down, preferred_element_type=F32)
            whole = whole.reshape(rows, n_seq, width).transpose(1, 0, 2)
            whole = jnp.take(whole, seq ^ jnp.array(masks, jnp.int32), axis=0)
            own, far = whole[:, :half], whole[:, half:].astype(BF16)
        total = own + hop(far, "tp", 1).astype(F32)
        for bit in seq_bits:
            count = total.shape[0] // 2
            total = total[:count] + hop(total[count:].astype(BF16), "seq", bit).astype(F32)
        part = total[0]
        for bit in [1 << b for b in range(1, n_tp.bit_length() - 1)]:
            sent = lax.reduce_precision(part, 8, 7)
            part = sent + hop(sent.astype(BF16), "tp", bit).astype(F32)
        own = (mixed + part).astype(BF16)
        far = hop(own, "tp", 1)
        first, second = jnp.where(core == 0, own, far), jnp.where(core == 0, far, own)
        result = jnp.concatenate([first, second], axis=0).reshape(steps, requests, width)
    return result, keys.reshape(key_cache.shape), values.reshape(value_cache.shape)


def solution(mesh):
    placed = (
        P(None, None, "seq"),
        P("seq"),
        P("seq", "tp"),
        P("seq", "tp"),
        P("seq", "tp"),
        P("tp", "seq"),
        P(),
        P(None, ("seq", "tp")),
        P(None, ("seq", "tp")),
        P(("seq", "tp"), None),
        P(None, "seq", "tp", None),
        P(None, "seq", "tp", None),
        P(),
    )
    return jax.shard_map(
        functools.partial(per_device, mesh.shape["seq"], mesh.shape["tp"]),
        mesh=mesh,
        in_specs=placed,
        out_specs=(P(None, None, "seq"), P(None, "seq", "tp", None), P(None, "seq", "tp", None)),
        check_vma=False,
    )
```

```python
import functools
import math

import jax
import jax.numpy as jnp
from jax import lax
from jax.experimental import pallas as pl
from jax.experimental.pallas import tpu as pltpu
from jax.sharding import PartitionSpec as P

F32 = jnp.float32
BF16 = jnp.bfloat16
LANES = 128
VMEM = pl.BlockSpec(memory_space=pltpu.VMEM)
SMEM = pl.BlockSpec(memory_space=pltpu.SMEM)
HBM = pl.BlockSpec(memory_space=pltpu.HBM)
ANY = pl.BlockSpec(memory_space=pl.ANY)


def call(body, outs, ins, scratch=(), cost=3, limit=8):
    return pl.pallas_call(
        body,
        out_shape=outs,
        in_specs=ins,
        out_specs=[VMEM] * len(outs),
        scratch_shapes=list(scratch),
        cost_estimate=pl.CostEstimate(flops=int(cost * 1.15e9), bytes_accessed=1 << 20, transcendentals=0),
        compiler_params=pltpu.CompilerParams(vmem_limit_bytes=limit << 20),
    )


def sds(shape, dtype):
    return jax.ShapeDtypeStruct(shape, dtype)


def lane_ids(rows):
    return lax.broadcasted_iota(jnp.int32, (rows, LANES), 1)


def split3(value):
    high = value.astype(BF16)
    rest = value - high.astype(F32)
    mid = rest.astype(BF16)
    low = (rest - mid.astype(F32)).astype(BF16)
    return high, mid, low


def pack_stats(stats):
    high, mid, low = (part.astype(F32) for part in split3(stats))
    return (high + pltpu.roll(mid, 8, 1) + pltpu.roll(low, 16, 1)).astype(BF16)


def unpack_stats(packed):
    packed = packed.astype(F32)
    return (packed + pltpu.roll(packed, LANES - 8, 1)) + pltpu.roll(packed, LANES - 16, 1)


def halves(x):
    steps, requests, _ = x.shape
    cut = requests // 2
    low = jnp.concatenate([x[t, :cut] for t in range(steps)], axis=0)
    high = jnp.concatenate([x[t, cut:] for t in range(steps)], axis=0)
    return low, high


def project_kernel(
    pair_ref,
    x_hbm,
    gain_hbm,
    wq_hbm,
    wk_hbm,
    wv_hbm,
    k_hbm,
    v_hbm,
    acc_ref,
    msg_ref,
    lent_ref,
    x_ref,
    gain_ref,
    wq_ref,
    wk_ref,
    wv_ref,
    sems,
):
    cut = lent_ref.shape[1]
    lent = pl.ds((1 - pair_ref[0]) * cut, cut)
    copies = [
        pltpu.make_async_copy(source, target, sems.at[i])
        for i, (source, target) in enumerate(
            (
                (x_hbm, x_ref),
                (gain_hbm, gain_ref),
                (wq_hbm, wq_ref),
                (wk_hbm, wk_ref),
                (wv_hbm, wv_ref),
                (k_hbm.at[lent], lent_ref.at[0]),
                (v_hbm.at[lent], lent_ref.at[1]),
            )
        )
    ]
    for copy in copies:
        copy.start()
    copies[0].wait()
    copies[1].wait()
    low, high = halves(x_ref[...].astype(F32))
    first = pair_ref[0] == 0
    x = jnp.concatenate([jnp.where(first, low, high), jnp.where(first, high, low)], axis=0)
    normed = (x * gain_ref[...].astype(F32)).astype(BF16)
    squares = jnp.sum(x * x, axis=1, keepdims=True)
    at = 0
    for copy, w_ref in zip(copies[2:], (wq_ref, wk_ref, wv_ref)):
        copy.wait()
        width = w_ref.shape[1]
        part = jnp.dot(normed, w_ref[...], preferred_element_type=F32)
        acc_ref[:, at : at + width] = part
        msg_ref[:, at : at + width] = part.astype(BF16)
        at += width
    stats = jnp.where(lane_ids(x.shape[0]) == 0, squares, 0.0)
    acc_ref[:, at:] = stats
    msg_ref[:, at:] = pack_stats(stats)
    copies[5].wait()
    copies[6].wait()


def added(acc_ref, recv_ref):
    at = acc_ref.shape[1] - LANES
    total = acc_ref[:, :at] + recv_ref[:, :at].astype(F32)
    stats = acc_ref[:, at:] + unpack_stats(recv_ref[:, at:])
    return total, jnp.where(lane_ids(stats.shape[0]) == 0, stats, 0.0)


def add_kernel(acc_ref, recv_ref, out_ref, msg_ref):
    at = acc_ref.shape[1] - LANES
    total, stats = added(acc_ref, recv_ref)
    out_ref[:, :at] = total
    msg_ref[:, :at] = total.astype(BF16)
    out_ref[:, at:] = stats
    msg_ref[:, at:] = pack_stats(stats)


def part_kernel(acc_ref, recv_ref, out_ref, msg_ref):
    at = acc_ref.shape[1] - LANES
    total, stats = added(acc_ref, recv_ref)
    half = total.shape[0] // 2
    out_ref[:, :at] = total[:half]
    msg_ref[:, :at] = total[half:].astype(BF16)
    out_ref[:, at:] = stats[:half]
    msg_ref[:, at:] = pack_stats(stats[half:])


def attend_kernel(
    heads,
    kv,
    steps,
    features,
    span,
    seq_ref,
    len_ref,
    acc_ref,
    recv_ref,
    cos_ref,
    sin_ref,
    k_ref,
    v_ref,
    far_ref,
    o_ref,
    st_ref,
    msg_ref,
    new_ref,
    q_buf,
    kn_buf,
    vn_buf,
    o_buf,
    m_buf,
    l_buf,
):
    requests, rows_kv, hd = far_ref.shape[1:]
    group = heads // kv
    block = steps * heads
    fresh = steps * kv
    at = (heads + 2 * kv) * hd
    squares = acc_ref[:, at:] + unpack_stats(recv_ref[:, at:])
    scale = lax.rsqrt(squares[:, 0:1] / features + 1e-05)

    def vector(index):
        cols = slice(index * hd, (index + 1) * hd)
        return (acc_ref[:, cols] + recv_ref[:, cols].astype(F32)) * scale

    def rotated(value):
        return value * cos_ref[...] + pltpu.roll(value, hd // 2, 1) * sin_ref[...]

    def spread(buf, value, index, per_step):
        for t in range(steps):
            buf[pl.ds(t * per_step + index, requests, stride=steps * per_step), :] = value[
                t * requests : (t + 1) * requests
            ]

    for g in range(kv):
        for i, (buf, value) in enumerate(
            ((kn_buf, rotated(vector(heads + g))), (vn_buf, vector(heads + kv + g)))
        ):
            spread(buf, value, g, kv)
            new_ref[:, (i * kv + g) * hd : (i * kv + g + 1) * hd] = value.astype(BF16)
    for h in range(heads):
        spread(q_buf, rotated(vector(h)), h, heads)

    seq = seq_ref[0]
    pair = seq & 1
    own_first = seq * span
    far_first = (seq ^ 1) * span
    low = (seq - pair) * span
    shrink = hd ** (-0.5)

    k_new = kn_buf[...].astype(BF16)
    v_new = vn_buf[...].astype(BF16)
    queries = q_buf[...].astype(BF16)
    shape = (requests * block, requests * fresh)
    row = lax.broadcasted_iota(jnp.int32, shape, 0)
    col = lax.broadcasted_iota(jnp.int32, shape, 1)
    col_row = lax.broadcasted_iota(jnp.int32, (1, shape[1]), 1)
    at_position = (col_row % fresh) // kv
    for r in range(requests):
        at_position += jnp.where(col_row // fresh == r, len_ref[pair * requests + r], 0)
    held = (at_position >= low) & (at_position < low + 2 * span)
    new_live = (
        (row // block == col // fresh)
        & ((row % heads) // group == col % kv)
        & ((row % block) // heads >= (col % fresh) // kv)
        & held
    )
    new_scores = (
        lax.dot_general(queries, k_new, (((1,), (1,)), ((), ())), preferred_element_type=F32) * shrink
    )
    new_scores = jnp.where(new_live, new_scores, -1e30)
    new_top = jnp.max(new_scores, axis=1, keepdims=True)

    row = lax.broadcasted_iota(jnp.int32, (block, rows_kv), 0)
    col = lax.broadcasted_iota(jnp.int32, (block, rows_kv), 1)
    need = jnp.where((row % heads) // group == col % kv, col // kv, 1 << 29)
    for r in range(requests):
        mine = slice(r * block, (r + 1) * block)
        query = queries[mine]
        length = len_ref[pair * requests + r]
        top = new_top[mine]
        parts = []
        for keys, first in ((k_ref[pair * requests + r], own_first), (far_ref[0, r], far_first)):
            scores = lax.dot_general(query, keys, (((1,), (1,)), ((), ())), preferred_element_type=F32) * shrink
            live = need < length - first
            masked = jnp.where(live, scores, -1e30)
            top = jnp.maximum(top, jnp.max(masked, axis=1, keepdims=True))
            parts.append((live, masked))
        total = jnp.zeros((block, 1), F32)
        summed = jnp.zeros((block, hd), F32)
        for (live, masked), values in zip(parts, (v_ref[pair * requests + r], far_ref[1, r])):
            expo = jnp.where(live, jnp.exp(masked - top), 0.0)
            total += jnp.sum(expo, axis=1, keepdims=True)
            summed += jnp.dot(expo.astype(BF16), values, preferred_element_type=F32)
        o_buf[mine, :] = summed
        m_buf[mine, :] = jnp.broadcast_to(top, (block, hd))
        l_buf[mine, :] = jnp.broadcast_to(total, (block, hd))
    expo = jnp.where(new_live, jnp.exp(new_scores - m_buf[:, 0:1]), 0.0)
    l_buf[...] += jnp.sum(expo, axis=1, keepdims=True)
    o_buf[...] += jnp.dot(expo.astype(BF16), v_new, preferred_element_type=F32)

    lane = lane_ids(requests)
    for t in range(steps):
        mine = slice(t * requests, (t + 1) * requests)
        stats = jnp.zeros((requests, LANES), F32)
        for h in range(heads):
            take = pl.ds(t * heads + h, requests, stride=block)
            o_ref[mine, h * hd : (h + 1) * hd] = o_buf[take, :]
            stats = jnp.where(lane == h, m_buf[take, :], stats)
            stats = jnp.where(lane == 24 + h, l_buf[take, :], stats)
        st_ref[mine, :] = stats
    msg_ref[:, : heads * hd] = o_ref[...].astype(BF16)
    msg_ref[:, heads * hd :] = pack_stats(st_ref[...])


def merged(heads, o_ref, st_ref, recv_ref):
    hd = o_ref.shape[1] // heads
    mine = st_ref[...]
    theirs = unpack_stats(recv_ref[:, heads * hd :])
    top = jnp.maximum(mine, theirs)
    keep, take = jnp.exp(mine - top), jnp.exp(theirs - top)
    total = mine * pltpu.roll(keep, 24, 1) + theirs * pltpu.roll(take, 24, 1)
    lane = lane_ids(mine.shape[0])
    stats = jnp.where(lane < heads, top, jnp.where((lane >= 24) & (lane < 24 + heads), total, 0.0))

    def head(h):
        cols = slice(h * hd, (h + 1) * hd)
        return o_ref[:, cols] * keep[:, h : h + 1] + recv_ref[:, cols].astype(F32) * take[:, h : h + 1]

    return stats, head


def merge_kernel(heads, o_ref, st_ref, recv_ref, o_out, st_out, msg_out):
    stats, head = merged(heads, o_ref, st_ref, recv_ref)
    hd = o_ref.shape[1] // heads
    for h in range(heads):
        value = head(h)
        o_out[:, h * hd : (h + 1) * hd] = value
        msg_out[:, h * hd : (h + 1) * hd] = value.astype(BF16)
    st_out[...] = stats
    msg_out[:, heads * hd :] = pack_stats(stats)


def finish_kernel(heads, o_ref, st_ref, recv_ref, new_ref, att_ref):
    stats, head = merged(heads, o_ref, st_ref, recv_ref)
    hd = o_ref.shape[1] // heads
    for h in range(heads):
        att_ref[:, h * hd : (h + 1) * hd] = (head(h) / stats[:, 24 + h : 25 + h]).astype(BF16)
    att_ref[:, heads * hd :] = new_ref[...]


def store_kernel(
    heads, steps, span, seq_ref, len_ref, own_ref, far_ref, k_ref, v_ref, after_ref, k_out, v_out, done_ref, buf
):
    done_ref[...] = after_ref[...]
    requests, rows_kv, hd = k_ref.shape
    kv = rows_kv // span
    cut = requests // 2
    fresh = steps * kv
    seq = seq_ref[0]
    low = (seq & 1) == 0
    place = lax.broadcasted_iota(jnp.int32, (rows_kv, fresh), 0) - lax.broadcasted_iota(
        jnp.int32, (rows_kv, fresh), 1
    )
    line = lax.broadcasted_iota(jnp.int32, (rows_kv, hd), 0)
    for i, (cache_ref, out_ref) in enumerate(((k_ref, k_out), (v_ref, v_out))):
        for g in range(kv):
            at = (heads + i * kv + g) * hd
            own, far = (ref[:, at : at + hd].astype(F32) for ref in (own_ref, far_ref))
            for n, value in enumerate((jnp.where(low, own, far), jnp.where(low, far, own))):
                for t in range(steps):
                    buf[pl.ds((i * 2 + n) * cut * fresh + t * kv + g, cut, stride=fresh), :] = value[
                        t * cut : (t + 1) * cut
                    ]
        out_ref[...] = cache_ref[...]
        for r in range(requests):
            base = (len_ref[r] - seq * span) * kv

            @pl.when((base > -fresh) & (base < rows_kv))
            def _():
                pick = jnp.where(place == base, 1.0, 0.0).astype(BF16)
                at = (i * requests + r) * fresh
                rows = buf[at : at + fresh, :].astype(BF16)
                put = jnp.dot(pick, rows, preferred_element_type=F32)
                new = (line >= base) & (line < base + fresh)
                out_ref[r] = jnp.where(new, put, cache_ref[r].astype(F32)).astype(BF16)


def mix_kernel(seq_ref, core_ref, own_ref, far_ref, w_ref, mine_ref, other_ref):
    depth = w_ref.shape[0]
    att = jnp.concatenate([own_ref[:, :depth], far_ref[:, :depth]], axis=0)
    part = jnp.dot(att, w_ref[...], preferred_element_type=F32)
    half = part.shape[0] // 2
    same = (seq_ref[0] & 1) == core_ref[0]
    mine_ref[...] = jnp.where(same, part[:half], part[half:])
    other_ref[...] = jnp.where(same, part[half:], part[:half])


def stack_kernel(ties, *refs):
    *in_refs, out_ref = refs[ties:]
    at = 0
    for ref in in_refs:
        out_ref[at : at + ref.shape[0]] = ref[...]
        at += ref.shape[0]


def round_kernel(mine_ref, recv_ref, msg_ref):
    msg_ref[...] = (mine_ref[...] + recv_ref[...]).astype(BF16)


def sum_kernel(mine_ref, recv_ref, msg_ref):
    msg_ref[...] = (mine_ref[...].astype(F32) + recv_ref[...].astype(F32)).astype(BF16)


def residual_kernel(core_ref, x_ref, gain_ref, mine_ref, recv_ref, mixed_ref, piece_ref):
    low, high = halves(x_ref[...].astype(F32))
    part = mine_ref[...].astype(F32) + recv_ref[...].astype(F32)
    mixed = jnp.where(core_ref[0] == 0, low, high) + part
    mixed_ref[...] = mixed
    squares = jnp.sum(mixed * mixed, axis=1, keepdims=True)
    stats = jnp.where(lane_ids(mixed.shape[0]) == 0, squares, 0.0)
    piece_ref[0, :, :LANES] = pack_stats(stats)
    piece_ref[0, :, LANES:] = (mixed * gain_ref[...].astype(F32)).astype(BF16)


def gather_products(masks, seq, own_ref, far_ref, wg_ref, wu_ref):
    count, width = own_ref.shape[0], own_ref.shape[2] - LANES
    squares = []
    for ref in (own_ref, far_ref):
        total = unpack_stats(ref[0, :, :LANES])
        for j in range(1, count):
            total += unpack_stats(ref[j, :, :LANES])
        squares.append(total)
    gate = up = 0.0
    for j in range(count):
        take = pl.ds(pl.multiple_of((seq ^ masks[j]) * width, 16), width)
        x = jnp.concatenate([own_ref[j, :, LANES:], far_ref[j, :, LANES:]], axis=0)
        gate += jnp.dot(x, wg_ref[take, :], preferred_element_type=F32)
        up += jnp.dot(x, wu_ref[take, :], preferred_element_type=F32)
    return jnp.concatenate(squares, axis=0), gate, up


def begin_kernel(masks, seq_ref, own_ref, far_ref, wg_ref, wu_ref, sq_ref, gate_ref, up_ref):
    squares, gate, up = gather_products(masks, seq_ref[0], own_ref, far_ref, wg_ref, wu_ref)
    sq_ref[...] = squares
    gate_ref[...] = gate
    up_ref[...] = up


def hidden_kernel(
    masks, features, seq_ref, own_ref, far_ref, wg_ref, wu_ref, sq_ref, gate_ref, up_ref, h_ref
):
    squares, gate, up = gather_products(masks, seq_ref[0], own_ref, far_ref, wg_ref, wu_ref)
    scale = lax.rsqrt((squares + sq_ref[...])[:, 0:1] / features + 1e-05)
    gate = (gate + gate_ref[...]) * scale
    up = (up + up_ref[...]) * scale
    h_ref[...] = (gate / (1.0 + jnp.exp(-gate)) * up).astype(BF16)


def down_kernel(masks, seq_ref, h_ref, w_ref, own_ref, far_ref):
    half, width = own_ref.shape[1:]
    hidden = h_ref[...]
    for j, mask in enumerate(masks):
        take = pl.ds(pl.multiple_of((seq_ref[0] ^ mask) * width, LANES), width)
        part = jnp.dot(hidden, w_ref[:, take], preferred_element_type=F32)
        own_ref[j] = part[:half]
        far_ref[j] = part[half:].astype(BF16)


def fold_kernel(acc_ref, *refs):
    *recv_refs, keep_ref, msg_ref = refs
    count = acc_ref.shape[0] // 2
    for j in range(2 * count):
        total = acc_ref[j]
        for ref in recv_refs:
            total += ref[j].astype(F32)
        if j < count:
            keep_ref[j] = total
        else:
            msg_ref[j - count] = total.astype(BF16)


def end_kernel(mixed_ref, mine_ref, recv_ref, out_ref):
    part = mine_ref[0].astype(F32) + recv_ref[0].astype(F32)
    out_ref[...] = (mixed_ref[...] + part).astype(BF16)


def join_kernel(core_ref, own_ref, far_ref, out_ref):
    steps, requests, _ = out_ref.shape
    cut = requests // 2
    low = core_ref[0] == 0
    own, far = own_ref[...].astype(F32), far_ref[...].astype(F32)
    first, second = jnp.where(low, own, far), jnp.where(low, far, own)
    for t in range(steps):
        rows = slice(t * cut, (t + 1) * cut)
        out_ref[t] = jnp.concatenate([first[rows], second[rows]], axis=0).astype(BF16)


def per_device(
    n_seq,
    n_tp,
    tokens,
    attn_gain,
    w_query,
    w_key,
    w_value,
    w_out,
    ffn_gain,
    w_gate,
    w_up,
    w_down,
    key_cache,
    value_cache,
    lengths,
):
    steps, requests, width = tokens.shape
    span, kv, hd = key_cache.shape[1:]
    heads = w_query.shape[1] // hd
    cut = requests // 2
    half = steps * cut
    features = width * n_seq
    hidden_width = w_gate.shape[1]
    wide = w_query.shape[1] + w_key.shape[1] + w_value.shape[1] + LANES
    seq = lax.axis_index("seq").astype(jnp.int32)
    pair = seq & 1
    core = lax.axis_index("tp").astype(jnp.int32) & 1
    seq_arr, core_arr, pair_arr = seq.reshape(1), core.reshape(1), pair.reshape(1)
    seq_bits = [1 << b for b in range(n_seq.bit_length() - 1)]
    tp_bits = [1 << b for b in range(n_tp.bit_length() - 1)]
    masks = [0]
    for bit in reversed(seq_bits):
        masks = masks + [m ^ bit for m in masks]
    near, away = masks[: n_seq // 2], masks[n_seq // 2 :]

    def hop(value, axis, bit):
        size = n_seq if axis == "seq" else n_tp
        return lax.ppermute(value, axis, [(i, i ^ bit) for i in range(size)])

    flat = (requests, span * kv, hd)
    k_flat, v_flat = key_cache.reshape(flat), value_cache.reshape(flat)
    with jax.named_scope("project"):
        rows = 2 * half
        acc, msg, lent = call(
            project_kernel,
            [sds((rows, wide), F32), sds((rows, wide), BF16), sds((2, cut) + flat[1:], BF16)],
            [SMEM] + [HBM] * 7,
            [
                pltpu.VMEM(tokens.shape, BF16),
                pltpu.VMEM(attn_gain.shape, BF16),
                pltpu.VMEM(w_query.shape, BF16),
                pltpu.VMEM(w_key.shape, BF16),
                pltpu.VMEM(w_value.shape, BF16),
                pltpu.SemaphoreType.DMA((7,)),
            ],
            limit=60,
        )(pair_arr, tokens, attn_gain, w_query, w_key, w_value, k_flat, v_flat)
        borrowed = hop(lent, "seq", 1)
        for bit in reversed(seq_bits[1:]):
            recv = hop(msg, "seq", bit)
            last = bit == seq_bits[1]
            count = half if last else rows
            acc, msg = call(
                part_kernel if last else add_kernel,
                [sds((count, wide), F32), sds((count, wide), BF16)],
                [VMEM] * 2,
            )(acc, recv)
        recv = hop(msg, "seq", 1)

    lent_lengths = lax.dynamic_slice_in_dim(lengths, pair * cut, cut, 0)
    positions = (lent_lengths[None, :] + jnp.arange(steps, dtype=jnp.int32)[:, None]).reshape(half)
    freqs = jnp.exp(jnp.arange(hd // 2, dtype=F32) * (-2.0 * math.log(100000000.0) / hd))
    angles = positions.astype(F32)[:, None] * freqs[None, :]
    cosine, sine = jnp.cos(angles), jnp.sin(angles)
    cosine = jnp.concatenate([cosine, cosine], axis=1)
    sine = jnp.concatenate([-sine, sine], axis=1)

    with jax.named_scope("attend"):
        block = steps * heads
        fresh = steps * kv
        joint = [
            sds((half, heads * hd), F32),
            sds((half, LANES), F32),
            sds((half, heads * hd + LANES), BF16),
        ]
        o, st, msg, news = call(
            functools.partial(attend_kernel, heads, kv, steps, features, span),
            joint + [sds((half, 2 * kv * hd), BF16)],
            [SMEM, SMEM] + [VMEM] * 7,
            [
                pltpu.VMEM((cut * block, hd), F32),
                pltpu.VMEM((cut * fresh, hd), F32),
                pltpu.VMEM((cut * fresh, hd), F32),
                pltpu.VMEM((cut * block, hd), F32),
                pltpu.VMEM((cut * block, hd), F32),
                pltpu.VMEM((cut * block, hd), F32),
            ],
        )(seq_arr, lengths, acc, recv, cosine, sine, k_flat, v_flat, borrowed)
        for bit in seq_bits[1:-1]:
            o, st, msg = call(functools.partial(merge_kernel, heads), joint, [VMEM] * 3)(
                o, st, hop(msg, "seq", bit)
            )
        (attended,) = call(
            functools.partial(finish_kernel, heads),
            [sds((half, (heads + 2 * kv) * hd), BF16)],
            [VMEM] * 4,
        )(o, st, hop(msg, "seq", seq_bits[-1]), news)
        others = hop(attended, "seq", 1)

    with jax.named_scope("mix"):
        mine, other = call(mix_kernel, [sds((half, width), F32)] * 2, [SMEM, SMEM] + [VMEM] * 3)(
            seq_arr, core_arr, attended, others, w_out
        )
        (part,) = call(round_kernel, [sds((half, width), BF16)], [VMEM] * 2)(mine, hop(other, "tp", 1))
        for bit in tp_bits[1:-1]:
            (part,) = call(sum_kernel, [sds((half, width), BF16)], [VMEM] * 2)(part, hop(part, "tp", bit))
        gain = lax.dynamic_slice_in_dim(ffn_gain, seq * width, width, 0).reshape(1, width)
        mixed, pieces = call(
            residual_kernel,
            [sds((half, width), F32), sds((1, half, LANES + width), BF16)],
            [SMEM] + [VMEM] * 4,
        )(core_arr, tokens, gain, part, hop(part, "tp", tp_bits[-1]))
        ties = []
        for bit in reversed(seq_bits[1:]):
            if bit == seq_bits[1]:
                keys, values, done = call(
                    functools.partial(store_kernel, heads, steps, span),
                    [sds(flat, BF16)] * 2 + [sds((half, LANES), F32)],
                    [SMEM, SMEM] + [VMEM] * 5,
                    [pltpu.VMEM((2 * requests * fresh, hd), F32)],
                )(seq_arr, lengths, attended, others, k_flat, v_flat, pieces[0, :, :LANES].astype(F32))
                ties = [done]
            more = hop(pieces, "seq", bit)
            (pieces,) = call(
                functools.partial(stack_kernel, len(ties)),
                [sds((2 * pieces.shape[0],) + pieces.shape[1:], BF16)],
                [VMEM] * (len(ties) + 2),
            )(*ties, pieces, more)

    with jax.named_scope("ffn"):
        more = hop(pieces, "seq", 1)
        partial_products = call(
            functools.partial(begin_kernel, near),
            [sds((rows, LANES), F32)] + [sds((rows, hidden_width), F32)] * 2,
            [SMEM] + [VMEM] * 4,
        )(seq_arr, pieces, hop(pieces, "tp", 1), w_gate, w_up)
        (hidden,) = call(
            functools.partial(hidden_kernel, away, features),
            [sds((rows, hidden_width), BF16)],
            [SMEM] + [VMEM] * 7,
        )(seq_arr, more, hop(more, "tp", 1), w_gate, w_up, *partial_products)

        def down(some):
            shape = (len(some), half, width)
            if width % LANES == 0:
                return call(
                    functools.partial(down_kernel, some),
                    [sds(shape, F32), sds(shape, BF16)],
                    [SMEM] + [VMEM] * 2,
                )(seq_arr, hidden, w_down)
            whole = jnp.dot(hidden, w_down, preferred_element_type=F32)
            whole = whole.reshape(rows, n_seq, width).transpose(1, 0, 2)
            whole = jnp.take(whole, seq ^ jnp.array(some, jnp.int32), axis=0)
            return whole[:, :half], whole[:, half:].astype(BF16)

        away_own, away_far = down(away)
        near_own, near_far = down(near)
        shape = (len(away), half, width)
        (msg,) = call(round_kernel, [sds(shape, BF16)], [VMEM] * 2)(
            away_own, hop(away_far, "tp", 1).astype(F32)
        )
        arrived = [hop(near_far, "tp", 1), hop(msg, "seq", 1)]
        keep = near_own
        for bit in seq_bits[1:]:
            shape = (keep.shape[0] // 2, half, width)
            keep, msg = call(fold_kernel, [sds(shape, F32), sds(shape, BF16)], [VMEM] * (1 + len(arrived)))(
                keep, *arrived
            )
            arrived = [hop(msg, "seq", bit)]
        shape = (1, half, width)
        (part,) = call(sum_kernel, [sds(shape, BF16)], [VMEM] * 2)(keep, arrived[0])
        for bit in tp_bits[1:-1]:
            (part,) = call(sum_kernel, [sds(shape, BF16)], [VMEM] * 2)(part, hop(part, "tp", bit))
        (own,) = call(end_kernel, [sds((half, width), BF16)], [VMEM] * 3)(
            mixed, part, hop(part, "tp", tp_bits[-1])
        )
        (result,) = call(join_kernel, [sds(tokens.shape, BF16)], [SMEM] + [VMEM] * 2)(
            core_arr, own, hop(own, "tp", 1)
        )
    return result, keys.reshape(key_cache.shape), values.reshape(value_cache.shape)


def solution(mesh):
    placed = (
        P(None, None, "seq"),
        P("seq"),
        P("seq", "tp"),
        P("seq", "tp"),
        P("seq", "tp"),
        P("tp", "seq"),
        P(),
        P(None, ("seq", "tp")),
        P(None, ("seq", "tp")),
        P(("seq", "tp"), None),
        P(None, "seq", "tp", None),
        P(None, "seq", "tp", None),
        P(),
    )
    return jax.shard_map(
        functools.partial(per_device, mesh.shape["seq"], mesh.shape["tp"]),
        mesh=mesh,
        in_specs=placed,
        out_specs=(P(None, None, "seq"), P(None, "seq", "tp", None), P(None, "seq", "tp", None)),
        check_vma=False,
    )
```

```python
import functools
import math

import jax
import jax.numpy as jnp
from jax import lax
from jax.experimental import pallas as pl
from jax.experimental.pallas import tpu as pltpu
from jax.sharding import PartitionSpec as P

F32 = jnp.float32
BF16 = jnp.bfloat16
LANES = 128
VMEM = pl.BlockSpec(memory_space=pltpu.VMEM)
SMEM = pl.BlockSpec(memory_space=pltpu.SMEM)
HBM = pl.BlockSpec(memory_space=pltpu.HBM)


def call(body, outs, ins, scratch=(), places=None, cost=3, limit=8):
    return pl.pallas_call(
        body,
        out_shape=outs,
        in_specs=ins,
        out_specs=places or [VMEM] * len(outs),
        scratch_shapes=list(scratch),
        cost_estimate=pl.CostEstimate(flops=int(cost * 1.15e9), bytes_accessed=1 << 20, transcendentals=0),
        compiler_params=pltpu.CompilerParams(vmem_limit_bytes=limit << 20),
    )


def sds(shape, dtype):
    return jax.ShapeDtypeStruct(shape, dtype)


def lane_ids(rows):
    return lax.broadcasted_iota(jnp.int32, (rows, LANES), 1)


def split3(value):
    high = value.astype(BF16)
    rest = value - high.astype(F32)
    mid = rest.astype(BF16)
    low = (rest - mid.astype(F32)).astype(BF16)
    return high, mid, low


def pack_stats(stats):
    high, mid, low = (part.astype(F32) for part in split3(stats))
    return (high + pltpu.roll(mid, 8, 1) + pltpu.roll(low, 16, 1)).astype(BF16)


def unpack_stats(packed):
    packed = packed.astype(F32)
    return (packed + pltpu.roll(packed, LANES - 8, 1)) + pltpu.roll(packed, LANES - 16, 1)


def halves(x):
    steps, requests, _ = x.shape
    cut = requests // 2
    low = jnp.concatenate([x[t, :cut] for t in range(steps)], axis=0)
    high = jnp.concatenate([x[t, cut:] for t in range(steps)], axis=0)
    return low, high


def project_kernel(
    pair_ref, x_hbm, gain_hbm, wq_hbm, wk_hbm, wv_hbm, acc_ref, msg_ref, x_ref, gain_ref, wq_ref, wk_ref, wv_ref, sems
):
    copies = [
        pltpu.make_async_copy(source, target, sems.at[i])
        for i, (source, target) in enumerate(
            (
                (x_hbm, x_ref),
                (gain_hbm, gain_ref),
                (wq_hbm, wq_ref),
                (wk_hbm, wk_ref),
                (wv_hbm, wv_ref),
            )
        )
    ]
    for copy in copies:
        copy.start()
    copies[0].wait()
    copies[1].wait()
    low, high = halves(x_ref[...].astype(F32))
    first = pair_ref[0] == 0
    x = jnp.concatenate([jnp.where(first, low, high), jnp.where(first, high, low)], axis=0)
    half = x.shape[0] // 2
    normed = (x * gain_ref[...].astype(F32)).astype(BF16)
    squares = jnp.sum(x * x, axis=1, keepdims=True)
    at = 0
    for copy, w_ref in zip(copies[2:], (wq_ref, wk_ref, wv_ref)):
        copy.wait()
        width = w_ref.shape[1]
        part = jnp.dot(normed, w_ref[...], preferred_element_type=F32)
        acc_ref[:, at : at + width] = part[:half]
        msg_ref[:, at : at + width] = part[half:].astype(BF16)
        at += width
    stats = jnp.where(lane_ids(2 * half) == 0, squares, 0.0)
    acc_ref[:, at:] = stats[:half]
    msg_ref[:, at:] = pack_stats(stats[half:])


def add_kernel(acc_ref, recv_ref, out_ref, msg_ref):
    at = acc_ref.shape[1] - LANES
    total = acc_ref[:, :at] + recv_ref[:, :at].astype(F32)
    out_ref[:, :at] = total
    msg_ref[:, :at] = total.astype(BF16)
    stats = acc_ref[:, at:] + unpack_stats(recv_ref[:, at:])
    stats = jnp.where(lane_ids(stats.shape[0]) == 0, stats, 0.0)
    out_ref[:, at:] = stats
    msg_ref[:, at:] = pack_stats(stats)


def rotate_kernel(heads, kv, hd, features, acc_ref, recv_ref, cos_ref, sin_ref, out_ref):
    at = (heads + 2 * kv) * hd
    squares = acc_ref[:, at:] + unpack_stats(recv_ref[:, at:])
    scale = lax.rsqrt(squares[:, 0:1] / features + 1e-05)
    for index in range(heads + 2 * kv):
        cols = slice(index * hd, (index + 1) * hd)
        value = (acc_ref[:, cols] + recv_ref[:, cols].astype(F32)) * scale
        if index < heads + kv:
            value = value * cos_ref[...] + pltpu.roll(value, hd // 2, 1) * sin_ref[...]
        out_ref[:, cols] = value.astype(BF16)


def attend_kernel(heads, kv, steps, span, far, seq_ref, len_ref, rows_ref, k_ref, v_ref, *refs):
    if far:
        o_own, st_own, o_ref, st_ref, msg_ref = refs[:5]
    else:
        o_ref, st_ref = refs[:2]
    q_buf, kn_buf, vn_buf, s_buf, o_buf, m_buf, l_buf = refs[-7:]
    requests, rows_kv, hd = k_ref.shape
    cut = requests // 2
    half = steps * cut
    group = heads // kv
    block = steps * heads
    fresh = steps * kv
    seq = seq_ref[0]
    first = seq * span
    pair = seq & 1
    head_request = ((1 - pair) if far else pair) * cut

    def spread(buf, index, place, per_step):
        value = rows_ref[:, index * hd : (index + 1) * hd].astype(F32)
        for t in range(steps):
            buf[pl.ds(t * per_step + place, cut, stride=steps * per_step), :] = value[t * cut : (t + 1) * cut]

    for h in range(heads):
        spread(q_buf, h, h, heads)
    for g in range(kv):
        spread(kn_buf, heads + g, g, kv)
        spread(vn_buf, heads + kv + g, g, kv)
    shrink = hd ** (-0.5)
    queries = q_buf[...].astype(BF16)

    row = lax.broadcasted_iota(jnp.int32, (block, rows_kv), 0)
    col = lax.broadcasted_iota(jnp.int32, (block, rows_kv), 1)
    need = jnp.where((row % heads) // group == col % kv, col // kv, 1 << 29)
    for r in range(cut):
        scores = lax.dot_general(
            queries[r * block : (r + 1) * block],
            k_ref[head_request + r],
            (((1,), (1,)), ((), ())),
            preferred_element_type=F32,
        )
        live = need < len_ref[head_request + r] - first
        s_buf[r * block : (r + 1) * block, :] = jnp.where(live, scores * shrink, -1e30)

    k_new = kn_buf[...].astype(BF16)
    v_new = vn_buf[...].astype(BF16)
    shape = (cut * block, cut * fresh)
    row = lax.broadcasted_iota(jnp.int32, shape, 0)
    col = lax.broadcasted_iota(jnp.int32, shape, 1)
    col_row = lax.broadcasted_iota(jnp.int32, (1, shape[1]), 1)
    at_position = (col_row % fresh) // kv - first
    for r in range(cut):
        at_position += jnp.where(col_row // fresh == r, len_ref[head_request + r], 0)
    held = (at_position >= 0) & (at_position < span)
    new_live = (
        (row // block == col // fresh)
        & ((row % heads) // group == col % kv)
        & ((row % block) // heads >= (col % fresh) // kv)
        & held
    )
    new_scores = lax.dot_general(queries, k_new, (((1,), (1,)), ((), ())), preferred_element_type=F32)
    new_scores = jnp.where(new_live, new_scores * shrink, -1e30)

    scores = s_buf[...]
    top = jnp.maximum(jnp.max(scores, axis=1, keepdims=True), jnp.max(new_scores, axis=1, keepdims=True))
    top = jnp.maximum(top, -1e29)
    expo = jnp.exp(scores - top)
    new_expo = jnp.exp(new_scores - top)
    total = jnp.sum(expo, axis=1, keepdims=True) + jnp.sum(new_expo, axis=1, keepdims=True)
    m_buf[...] = jnp.broadcast_to(top, m_buf.shape)
    l_buf[...] = jnp.broadcast_to(total, l_buf.shape)
    expo = expo.astype(BF16)
    new_part = jnp.dot(new_expo.astype(BF16), v_new, preferred_element_type=F32)
    for r in range(cut):
        mine = slice(r * block, (r + 1) * block)
        o_buf[mine, :] = new_part[mine] + jnp.dot(
            expo[mine], v_ref[head_request + r], preferred_element_type=F32
        )

    lane = lane_ids(cut)
    base = pl.multiple_of((1 - pair) * half, half) if far else 0
    for t in range(steps):
        mine = pl.ds(base + t * cut, cut)
        stats = jnp.zeros((cut, LANES), F32)
        for h in range(heads):
            take = pl.ds(t * heads + h, cut, stride=block)
            o_ref[mine, h * hd : (h + 1) * hd] = o_buf[take, :]
            stats = jnp.where(lane == h, m_buf[take, :], stats)
            stats = jnp.where(lane == 24 + h, l_buf[take, :], stats)
        st_ref[mine, :] = stats
    if far:
        mine = pl.ds(pl.multiple_of(pair * half, half), half)
        o_ref[mine, :] = o_own[...]
        st_ref[mine, :] = st_own[...]
        msg_ref[:, : heads * hd] = o_ref[...].astype(BF16)
        msg_ref[:, heads * hd :] = pack_stats(st_ref[...])


def merged(heads, o_ref, st_ref, recv_ref):
    hd = o_ref.shape[1] // heads
    mine = st_ref[...]
    theirs = unpack_stats(recv_ref[:, heads * hd :])
    top = jnp.maximum(mine, theirs)
    keep, take = jnp.exp(mine - top), jnp.exp(theirs - top)
    total = mine * pltpu.roll(keep, 24, 1) + theirs * pltpu.roll(take, 24, 1)
    lane = lane_ids(mine.shape[0])
    stats = jnp.where(lane < heads, top, jnp.where((lane >= 24) & (lane < 24 + heads), total, 0.0))

    def head(h):
        cols = slice(h * hd, (h + 1) * hd)
        return o_ref[:, cols] * keep[:, h : h + 1] + recv_ref[:, cols].astype(F32) * take[:, h : h + 1]

    return stats, head


def merge_kernel(heads, o_ref, st_ref, recv_ref, o_out, st_out, msg_out):
    stats, head = merged(heads, o_ref, st_ref, recv_ref)
    hd = o_ref.shape[1] // heads
    for h in range(heads):
        value = head(h)
        o_out[:, h * hd : (h + 1) * hd] = value
        msg_out[:, h * hd : (h + 1) * hd] = value.astype(BF16)
    st_out[...] = stats
    msg_out[:, heads * hd :] = pack_stats(stats)


def store_kernel(
    heads, steps, span, seq_ref, len_ref, own_ref, far_ref, k_ref, v_ref, after_ref, k_out, v_out, done_ref, buf, win, sems
):
    done_ref[...] = after_ref[...]
    requests, rows_kv, hd = k_ref.shape
    span_rows = win.shape[2]
    kv = rows_kv // span
    cut = requests // 2
    fresh = steps * kv
    seq = seq_ref[0]
    low = (seq & 1) == 0
    caches = ((k_ref, k_out), (v_ref, v_out))
    whole = [pltpu.make_async_copy(c_ref, c_out, sems.at[i, requests]) for i, (c_ref, c_out) in enumerate(caches)]
    for copy in whole:
        copy.start()
    for i in range(2):
        for g in range(kv):
            at = (heads + i * kv + g) * hd
            own, far = (ref[:, at : at + hd].astype(F32) for ref in (own_ref, far_ref))
            for n, value in enumerate((jnp.where(low, own, far), jnp.where(low, far, own))):
                for t in range(steps):
                    buf[pl.ds((i * 2 + n) * cut * fresh + t * kv + g, cut, stride=fresh), :] = value[
                        t * cut : (t + 1) * cut
                    ]
    line = lax.broadcasted_iota(jnp.int32, (span_rows, hd), 0)
    place = lax.broadcasted_iota(jnp.int32, (span_rows, fresh), 0) - lax.broadcasted_iota(
        jnp.int32, (span_rows, fresh), 1
    )
    pieces = []
    for r in range(requests):
        base = (len_ref[r] - seq * span) * kv
        start = pl.multiple_of(jnp.clip((base // 16) * 16, 0, rows_kv - span_rows), 16)
        touched = (base > -fresh) & (base < rows_kv)
        pieces.append((touched, start))

        @pl.when(touched)
        def _():
            pick = jnp.where(place == base - start, 1.0, 0.0).astype(BF16)
            new = (line >= base - start) & (line < base - start + fresh)
            for i, (c_ref, _) in enumerate(caches):
                at = (i * requests + r) * fresh
                put = jnp.dot(pick, buf[at : at + fresh, :].astype(BF16), preferred_element_type=F32)
                old = c_ref[r, pl.ds(start, span_rows), :].astype(F32)
                win[i, r] = jnp.where(new, put, old).astype(BF16)

    for copy in whole:
        copy.wait()
    for act in ("start", "wait"):
        for r, (touched, start) in enumerate(pieces):

            @pl.when(touched)
            def _():
                for i, (_, c_out) in enumerate(caches):
                    copy = pltpu.make_async_copy(
                        win.at[i, r], c_out.at[r, pl.ds(start, span_rows), :], sems.at[i, r]
                    )
                    getattr(copy, act)()


def mix_kernel(heads, core_ref, o_ref, st_ref, recv_ref, w_ref, done_ref, mine_ref, other_ref, att_buf):
    stats, head = merged(heads, o_ref, st_ref, recv_ref)
    hd = o_ref.shape[1] // heads
    for h in range(heads):
        att_buf[:, h * hd : (h + 1) * hd] = (head(h) / stats[:, 24 + h : 25 + h]).astype(BF16)
    part = jnp.dot(att_buf[...], w_ref[...], preferred_element_type=F32)
    half = part.shape[0] // 2
    low = core_ref[0] == 0
    mine_ref[...] = jnp.where(low, part[:half], part[half:])
    other_ref[...] = jnp.where(low, part[half:], part[:half])


def stack_kernel(*refs):
    *in_refs, out_ref = refs
    at = 0
    for ref in in_refs:
        out_ref[at : at + ref.shape[0]] = ref[...]
        at += ref.shape[0]


def round_kernel(mine_ref, recv_ref, msg_ref):
    msg_ref[...] = (mine_ref[...] + recv_ref[...]).astype(BF16)


def sum_kernel(mine_ref, recv_ref, msg_ref):
    msg_ref[...] = (mine_ref[...].astype(F32) + recv_ref[...].astype(F32)).astype(BF16)


def residual_kernel(core_ref, x_ref, gain_ref, mine_ref, recv_ref, mixed_ref, piece_ref):
    low, high = halves(x_ref[...].astype(F32))
    part = mine_ref[...].astype(F32) + recv_ref[...].astype(F32)
    mixed = jnp.where(core_ref[0] == 0, low, high) + part
    mixed_ref[...] = mixed
    squares = jnp.sum(mixed * mixed, axis=1, keepdims=True)
    stats = jnp.where(lane_ids(mixed.shape[0]) == 0, squares, 0.0)
    piece_ref[0, :, :LANES] = pack_stats(stats)
    piece_ref[0, :, LANES:] = (mixed * gain_ref[...].astype(F32)).astype(BF16)


def gather_products(masks, seq, own_ref, far_ref, wg_ref, wu_ref):
    count, width = own_ref.shape[0], own_ref.shape[2] - LANES
    squares = []
    for ref in (own_ref, far_ref):
        total = unpack_stats(ref[0, :, :LANES])
        for j in range(1, count):
            total += unpack_stats(ref[j, :, :LANES])
        squares.append(total)
    gate = up = 0.0
    for j in range(count):
        take = pl.ds(pl.multiple_of((seq ^ masks[j]) * width, 16), width)
        x = jnp.concatenate([own_ref[j, :, LANES:], far_ref[j, :, LANES:]], axis=0)
        gate += jnp.dot(x, wg_ref[take, :], preferred_element_type=F32)
        up += jnp.dot(x, wu_ref[take, :], preferred_element_type=F32)
    return jnp.concatenate(squares, axis=0), gate, up


def begin_kernel(masks, seq_ref, own_ref, far_ref, wg_ref, wu_ref, sq_ref, gate_ref, up_ref):
    squares, gate, up = gather_products(masks, seq_ref[0], own_ref, far_ref, wg_ref, wu_ref)
    sq_ref[...] = squares
    gate_ref[...] = gate
    up_ref[...] = up


def hidden_kernel(
    masks, features, seq_ref, own_ref, far_ref, wg_ref, wu_ref, sq_ref, gate_ref, up_ref, h_ref
):
    squares, gate, up = gather_products(masks, seq_ref[0], own_ref, far_ref, wg_ref, wu_ref)
    scale = lax.rsqrt((squares + sq_ref[...])[:, 0:1] / features + 1e-05)
    gate = (gate + gate_ref[...]) * scale
    up = (up + up_ref[...]) * scale
    h_ref[...] = (gate / (1.0 + jnp.exp(-gate)) * up).astype(BF16)


def down_kernel(masks, seq_ref, h_ref, w_ref, own_ref, far_ref):
    half, width = own_ref.shape[1:]
    hidden = h_ref[...]
    for j, mask in enumerate(masks):
        take = pl.ds(pl.multiple_of((seq_ref[0] ^ mask) * width, LANES), width)
        part = jnp.dot(hidden, w_ref[:, take], preferred_element_type=F32)
        own_ref[j] = part[:half]
        far_ref[j] = part[half:].astype(BF16)


def fold_kernel(acc_ref, *refs):
    *recv_refs, keep_ref, msg_ref = refs
    count = acc_ref.shape[0] // 2
    for j in range(2 * count):
        total = acc_ref[j]
        for ref in recv_refs:
            total += ref[j].astype(F32)
        if j < count:
            keep_ref[j] = total
        else:
            msg_ref[j - count] = total.astype(BF16)


def end_kernel(mixed_ref, mine_ref, recv_ref, out_ref):
    part = mine_ref[0].astype(F32) + recv_ref[0].astype(F32)
    out_ref[...] = (mixed_ref[...] + part).astype(BF16)


def join_kernel(core_ref, own_ref, far_ref, out_ref):
    steps, requests, _ = out_ref.shape
    cut = requests // 2
    low = core_ref[0] == 0
    own, far = own_ref[...].astype(F32), far_ref[...].astype(F32)
    first, second = jnp.where(low, own, far), jnp.where(low, far, own)
    for t in range(steps):
        rows = slice(t * cut, (t + 1) * cut)
        out_ref[t] = jnp.concatenate([first[rows], second[rows]], axis=0).astype(BF16)


def per_device(
    n_seq,
    n_tp,
    tokens,
    attn_gain,
    w_query,
    w_key,
    w_value,
    w_out,
    ffn_gain,
    w_gate,
    w_up,
    w_down,
    key_cache,
    value_cache,
    lengths,
):
    steps, requests, width = tokens.shape
    span, kv, hd = key_cache.shape[1:]
    heads = w_query.shape[1] // hd
    cut = requests // 2
    half = steps * cut
    features = width * n_seq
    hidden_width = w_gate.shape[1]
    wide = w_query.shape[1] + w_key.shape[1] + w_value.shape[1] + LANES
    seq = lax.axis_index("seq").astype(jnp.int32)
    pair = seq & 1
    core = lax.axis_index("tp").astype(jnp.int32) & 1
    seq_arr, core_arr, pair_arr = seq.reshape(1), core.reshape(1), pair.reshape(1)
    seq_bits = [1 << b for b in range(n_seq.bit_length() - 1)]
    tp_bits = [1 << b for b in range(n_tp.bit_length() - 1)]
    masks = [0]
    for bit in reversed(seq_bits):
        masks = masks + [m ^ bit for m in masks]
    near, away = masks[: n_seq // 2], masks[n_seq // 2 :]

    def hop(value, axis, bit):
        size = n_seq if axis == "seq" else n_tp
        return lax.ppermute(value, axis, [(i, i ^ bit) for i in range(size)])

    flat = (requests, span * kv, hd)
    k_flat, v_flat = key_cache.reshape(flat), value_cache.reshape(flat)
    half_lengths = lax.dynamic_slice_in_dim(lengths, pair * cut, cut, 0)
    positions = (half_lengths[None, :] + jnp.arange(steps, dtype=jnp.int32)[:, None]).reshape(half)
    freqs = jnp.exp(jnp.arange(hd // 2, dtype=F32) * (-2.0 * math.log(100000000.0) / hd))
    angles = positions.astype(F32)[:, None] * freqs[None, :]
    cosine, sine = jnp.cos(angles), jnp.sin(angles)
    cosine = jnp.concatenate([cosine, cosine], axis=1)
    sine = jnp.concatenate([-sine, sine], axis=1)

    rows = 2 * half
    with jax.named_scope("project"):
        sums = [sds((half, wide), F32), sds((half, wide), BF16)]
        acc, msg = call(
            project_kernel,
            sums,
            [SMEM] + [HBM] * 5,
            [
                pltpu.VMEM(tokens.shape, BF16),
                pltpu.VMEM(attn_gain.shape, BF16),
                pltpu.VMEM(w_query.shape, BF16),
                pltpu.VMEM(w_key.shape, BF16),
                pltpu.VMEM(w_value.shape, BF16),
                pltpu.SemaphoreType.DMA((5,)),
            ],
            limit=60,
        )(pair_arr, tokens, attn_gain, w_query, w_key, w_value)
        recv = hop(msg, "seq", 1)
        for bit in seq_bits[1:]:
            acc, msg = call(add_kernel, sums, [VMEM] * 2)(acc, recv)
            recv = hop(msg, "seq", bit)
        (finished,) = call(
            functools.partial(rotate_kernel, heads, kv, hd, features),
            [sds((half, wide - LANES), BF16)],
            [VMEM] * 4,
        )(acc, recv, cosine, sine)
        others = hop(finished, "seq", 1)

    with jax.named_scope("attend"):
        block = steps * heads
        fresh = steps * kv
        joint = [
            sds((rows, heads * hd), F32),
            sds((rows, LANES), F32),
            sds((rows, heads * hd + LANES), BF16),
        ]
        scratch = [
            pltpu.VMEM((cut * block, hd), F32),
            pltpu.VMEM((cut * fresh, hd), F32),
            pltpu.VMEM((cut * fresh, hd), F32),
            pltpu.VMEM((cut * block, flat[1]), F32),
            pltpu.VMEM((cut * block, hd), F32),
            pltpu.VMEM((cut * block, hd), F32),
            pltpu.VMEM((cut * block, hd), F32),
        ]
        own = call(
            functools.partial(attend_kernel, heads, kv, steps, span, False),
            [sds((half, heads * hd), F32), sds((half, LANES), F32)],
            [SMEM, SMEM] + [VMEM] * 3,
            scratch,
        )(seq_arr, lengths, finished, k_flat, v_flat)
        o, st, msg = call(
            functools.partial(attend_kernel, heads, kv, steps, span, True),
            joint,
            [SMEM, SMEM] + [VMEM] * 5,
            scratch,
        )(seq_arr, lengths, others, k_flat, v_flat, *own)
        for bit in seq_bits[:-1]:
            o, st, msg = call(functools.partial(merge_kernel, heads), joint, [VMEM] * 3)(
                o, st, hop(msg, "seq", bit)
            )
        keys, values, done = call(
            functools.partial(store_kernel, heads, steps, span),
            [sds(flat, BF16)] * 2 + [sds((rows, LANES), F32)],
            [SMEM, SMEM] + [VMEM] * 5,
            [
                pltpu.VMEM((2 * requests * fresh, hd), F32),
                pltpu.VMEM((2, requests, 16 + -(-fresh // 16) * 16, hd), BF16),
                pltpu.SemaphoreType.DMA((2, requests + 1)),
            ],
            [HBM, HBM, VMEM],
        )(seq_arr, lengths, finished, others, k_flat, v_flat, st)
        recv = hop(msg, "seq", seq_bits[-1])

    with jax.named_scope("mix"):
        mine, other = call(
            functools.partial(mix_kernel, heads),
            [sds((half, width), F32)] * 2,
            [SMEM] + [VMEM] * 5,
            [pltpu.VMEM((rows, heads * hd), BF16)],
        )(core_arr, o, st, recv, w_out, done)
        (part,) = call(round_kernel, [sds((half, width), BF16)], [VMEM] * 2)(mine, hop(other, "tp", 1))
        for bit in tp_bits[1:-1]:
            (part,) = call(sum_kernel, [sds((half, width), BF16)], [VMEM] * 2)(part, hop(part, "tp", bit))
        gain = lax.dynamic_slice_in_dim(ffn_gain, seq * width, width, 0).reshape(1, width)
        mixed, pieces = call(
            residual_kernel,
            [sds((half, width), F32), sds((1, half, LANES + width), BF16)],
            [SMEM] + [VMEM] * 4,
        )(core_arr, tokens, gain, part, hop(part, "tp", tp_bits[-1]))
        for bit in reversed(seq_bits[1:]):
            more = hop(pieces, "seq", bit)
            (pieces,) = call(
                stack_kernel, [sds((2 * pieces.shape[0],) + pieces.shape[1:], BF16)], [VMEM] * 2
            )(pieces, more)

    with jax.named_scope("ffn"):
        more = hop(pieces, "seq", 1)
        partial_products = call(
            functools.partial(begin_kernel, near),
            [sds((rows, LANES), F32)] + [sds((rows, hidden_width), F32)] * 2,
            [SMEM] + [VMEM] * 4,
        )(seq_arr, pieces, hop(pieces, "tp", 1), w_gate, w_up)
        (hidden,) = call(
            functools.partial(hidden_kernel, away, features),
            [sds((rows, hidden_width), BF16)],
            [SMEM] + [VMEM] * 7,
        )(seq_arr, more, hop(more, "tp", 1), w_gate, w_up, *partial_products)

        def down(some):
            shape = (len(some), half, width)
            if width % LANES == 0:
                return call(
                    functools.partial(down_kernel, some),
                    [sds(shape, F32), sds(shape, BF16)],
                    [SMEM] + [VMEM] * 2,
                )(seq_arr, hidden, w_down)
            whole = jnp.dot(hidden, w_down, preferred_element_type=F32)
            whole = whole.reshape(rows, n_seq, width).transpose(1, 0, 2)
            whole = jnp.take(whole, seq ^ jnp.array(some, jnp.int32), axis=0)
            return whole[:, :half], whole[:, half:].astype(BF16)

        away_own, away_far = down(away)
        near_own, near_far = down(near)
        shape = (len(away), half, width)
        (msg,) = call(round_kernel, [sds(shape, BF16)], [VMEM] * 2)(
            away_own, hop(away_far, "tp", 1).astype(F32)
        )
        arrived = [hop(near_far, "tp", 1), hop(msg, "seq", 1)]
        keep = near_own
        for bit in seq_bits[1:]:
            shape = (keep.shape[0] // 2, half, width)
            keep, msg = call(fold_kernel, [sds(shape, F32), sds(shape, BF16)], [VMEM] * (1 + len(arrived)))(
                keep, *arrived
            )
            arrived = [hop(msg, "seq", bit)]
        shape = (1, half, width)
        (part,) = call(sum_kernel, [sds(shape, BF16)], [VMEM] * 2)(keep, arrived[0])
        for bit in tp_bits[1:-1]:
            (part,) = call(sum_kernel, [sds(shape, BF16)], [VMEM] * 2)(part, hop(part, "tp", bit))
        (own,) = call(end_kernel, [sds((half, width), BF16)], [VMEM] * 3)(
            mixed, part, hop(part, "tp", tp_bits[-1])
        )
        (result,) = call(join_kernel, [sds(tokens.shape, BF16)], [SMEM] + [VMEM] * 2)(
            core_arr, own, hop(own, "tp", 1)
        )
    return result, keys.reshape(key_cache.shape), values.reshape(value_cache.shape)


def solution(mesh):
    placed = (
        P(None, None, "seq"),
        P("seq"),
        P("seq", "tp"),
        P("seq", "tp"),
        P("seq", "tp"),
        P("tp", "seq"),
        P(),
        P(None, ("seq", "tp")),
        P(None, ("seq", "tp")),
        P(("seq", "tp"), None),
        P(None, "seq", "tp", None),
        P(None, "seq", "tp", None),
        P(),
    )
    return jax.shard_map(
        functools.partial(per_device, mesh.shape["seq"], mesh.shape["tp"]),
        mesh=mesh,
        in_specs=placed,
        out_specs=(P(None, None, "seq"), P(None, "seq", "tp", None), P(None, "seq", "tp", None)),
        check_vma=False,
    )
```

```python
import functools
import math

import jax
import jax.numpy as jnp
from jax import lax
from jax.experimental import pallas as pl
from jax.experimental.pallas import tpu as pltpu
from jax.sharding import PartitionSpec as P

F32 = jnp.float32
BF16 = jnp.bfloat16
LANES = 128
VMEM = pl.BlockSpec(memory_space=pltpu.VMEM)
SMEM = pl.BlockSpec(memory_space=pltpu.SMEM)
HBM = pl.BlockSpec(memory_space=pltpu.HBM)


def call(body, outs, ins, scratch=(), places=None, cost=3, limit=8):
    return pl.pallas_call(
        body,
        out_shape=outs,
        in_specs=ins,
        out_specs=places or [VMEM] * len(outs),
        scratch_shapes=list(scratch),
        cost_estimate=pl.CostEstimate(flops=int(cost * 1.15e9), bytes_accessed=1 << 20, transcendentals=0),
        compiler_params=pltpu.CompilerParams(vmem_limit_bytes=int(limit * 2**20)),
    )


def sds(shape, dtype):
    return jax.ShapeDtypeStruct(shape, dtype)


def lane_ids(rows):
    return lax.broadcasted_iota(jnp.int32, (rows, LANES), 1)


def split3(value):
    high = value.astype(BF16)
    rest = value - high.astype(F32)
    mid = rest.astype(BF16)
    low = (rest - mid.astype(F32)).astype(BF16)
    return high, mid, low


def pack_stats(stats):
    high, mid, low = (part.astype(F32) for part in split3(stats))
    return (high + pltpu.roll(mid, 8, 1) + pltpu.roll(low, 16, 1)).astype(BF16)


def unpack_stats(packed):
    packed = packed.astype(F32)
    return (packed + pltpu.roll(packed, LANES - 8, 1)) + pltpu.roll(packed, LANES - 16, 1)


def reorder(rows, source, x):
    shape = (rows, x.shape[0])
    row = lax.broadcasted_iota(jnp.int32, shape, 0)
    col = lax.broadcasted_iota(jnp.int32, shape, 1)
    pick = jnp.where(col == source(row), 1.0, 0.0).astype(BF16)
    return jnp.dot(pick, x, preferred_element_type=F32)


def project_kernel(
    steps,
    seq_ref,
    x_hbm,
    gain_hbm,
    wq_hbm,
    wk_hbm,
    wv_hbm,
    acc_ref,
    msg1_ref,
    msg2_ref,
    msg3_ref,
    x_ref,
    gain_ref,
    wq_ref,
    wk_ref,
    wv_ref,
    sems,
):
    copies = [
        pltpu.make_async_copy(source, target, sems.at[i])
        for i, (source, target) in enumerate(
            (
                (x_hbm, x_ref),
                (gain_hbm, gain_ref),
                (wq_hbm, wq_ref),
                (wk_hbm, wk_ref),
                (wv_hbm, wv_ref),
            )
        )
    ]
    for copy in copies:
        copy.start()
    copies[0].wait()
    copies[1].wait()
    rows = x_ref.shape[0]
    requests = rows // steps
    cut = requests // 4
    part = rows // 4
    place = seq_ref[0] & 3

    def source(row):
        return row % steps * requests + ((row // part) ^ place) * cut + row % part // steps

    x = reorder(rows, source, x_ref[...])
    normed = (x * gain_ref[...].astype(F32)).astype(BF16)
    squares = jnp.sum(x * x, axis=1, keepdims=True)
    msgs = (msg1_ref, msg2_ref, msg3_ref)
    at = 0
    for copy, w_ref in zip(copies[2:], (wq_ref, wk_ref, wv_ref)):
        copy.wait()
        width = w_ref.shape[1]
        product = jnp.dot(normed, w_ref[...], preferred_element_type=F32)
        acc_ref[:, at : at + width] = product[:part]
        for j, ref in enumerate(msgs):
            ref[:, at : at + width] = product[(j + 1) * part : (j + 2) * part].astype(BF16)
        at += width
    stats = jnp.where(lane_ids(rows) == 0, squares, 0.0)
    acc_ref[:, at:] = stats[:part]
    packed = pack_stats(stats)
    for j, ref in enumerate(msgs):
        ref[:, at:] = packed[(j + 1) * part : (j + 2) * part]


def keep_kernel(in_ref, out_ref):
    out_ref[...] = in_ref[...]


def add_kernel(acc_ref, *refs):
    *recv_refs, out_ref, msg_ref = refs
    at = acc_ref.shape[1] - LANES
    total, stats = acc_ref[:, :at], acc_ref[:, at:]
    for ref in recv_refs:
        total += ref[:, :at].astype(F32)
        stats += unpack_stats(ref[:, at:])
    stats = jnp.where(lane_ids(stats.shape[0]) == 0, stats, 0.0)
    out_ref[:, :at] = total
    msg_ref[:, :at] = total.astype(BF16)
    out_ref[:, at:] = stats
    msg_ref[:, at:] = pack_stats(stats)


def rotate_kernel(heads, kv, hd, features, acc_ref, recv_ref, cos_ref, sin_ref, out_ref):
    at = (heads + 2 * kv) * hd
    squares = acc_ref[:, at:] + unpack_stats(recv_ref[:, at:])
    scale = lax.rsqrt(squares[:, 0:1] / features + 1e-05)
    for index in range(heads + 2 * kv):
        cols = slice(index * hd, (index + 1) * hd)
        value = (acc_ref[:, cols] + recv_ref[:, cols].astype(F32)) * scale
        if index < heads + kv:
            value = value * cos_ref[...] + pltpu.roll(value, hd // 2, 1) * sin_ref[...]
        out_ref[:, cols] = value.astype(BF16)


def attend_kernel(heads, kv, steps, span, slot, seq_ref, len_ref, rows_ref, k_ref, v_ref, *refs):
    q_buf, kn_buf, vn_buf, s_buf, o_buf, m_buf, l_buf, o_all, st_all = refs[-9:]
    if slot == 0:
        o_all, st_all = refs[:2]
    requests, rows_kv, hd = k_ref.shape
    cut = requests // 4
    group = heads // kv
    block = steps * heads
    fresh = steps * kv
    seq = seq_ref[0]
    first = seq * span
    head_request = ((seq & 3) ^ slot) * cut

    def spread(buf, index, place, per_step):
        value = rows_ref[:, index * hd : (index + 1) * hd].astype(F32)
        buf[pl.ds(place, cut * steps, stride=per_step), :] = value

    for h in range(heads):
        spread(q_buf, h, h, heads)
    for g in range(kv):
        spread(kn_buf, heads + g, g, kv)
        spread(vn_buf, heads + kv + g, g, kv)
    shrink = hd ** (-0.5)
    queries = q_buf[...].astype(BF16)

    row = lax.broadcasted_iota(jnp.int32, (block, rows_kv), 0)
    col = lax.broadcasted_iota(jnp.int32, (block, rows_kv), 1)
    need = jnp.where((row % heads) // group == col % kv, col // kv, 1 << 29)
    for r in range(cut):
        scores = lax.dot_general(
            queries[r * block : (r + 1) * block],
            k_ref[head_request + r],
            (((1,), (1,)), ((), ())),
            preferred_element_type=F32,
        )
        live = need < len_ref[head_request + r] - first
        s_buf[r * block : (r + 1) * block, :] = jnp.where(live, scores * shrink, -1e30)

    k_new = kn_buf[...].astype(BF16)
    v_new = vn_buf[...].astype(BF16)
    shape = (cut * block, cut * fresh)
    row = lax.broadcasted_iota(jnp.int32, shape, 0)
    col = lax.broadcasted_iota(jnp.int32, shape, 1)
    col_row = lax.broadcasted_iota(jnp.int32, (1, shape[1]), 1)
    at_position = (col_row % fresh) // kv - first
    for r in range(cut):
        at_position += jnp.where(col_row // fresh == r, len_ref[head_request + r], 0)
    held = (at_position >= 0) & (at_position < span)
    new_live = (
        (row // block == col // fresh)
        & ((row % heads) // group == col % kv)
        & ((row % block) // heads >= (col % fresh) // kv)
        & held
    )
    new_scores = lax.dot_general(queries, k_new, (((1,), (1,)), ((), ())), preferred_element_type=F32)
    new_scores = jnp.where(new_live, new_scores * shrink, -1e30)

    scores = s_buf[...]
    top = jnp.maximum(jnp.max(scores, axis=1, keepdims=True), jnp.max(new_scores, axis=1, keepdims=True))
    top = jnp.maximum(top, -1e29)
    expo = jnp.exp(scores - top)
    new_expo = jnp.exp(new_scores - top)
    total = jnp.sum(expo, axis=1, keepdims=True) + jnp.sum(new_expo, axis=1, keepdims=True)
    m_buf[...] = jnp.broadcast_to(top, m_buf.shape)
    l_buf[...] = jnp.broadcast_to(total, l_buf.shape)
    expo = expo.astype(BF16)
    new_part = jnp.dot(new_expo.astype(BF16), v_new, preferred_element_type=F32)
    for r in range(cut):
        mine = slice(r * block, (r + 1) * block)
        o_buf[mine, :] = new_part[mine] + jnp.dot(
            expo[mine], v_ref[head_request + r], preferred_element_type=F32
        )

    lane = lane_ids(cut * steps)
    stats = jnp.zeros((cut * steps, LANES), F32)
    for h in range(heads):
        take = pl.ds(h, cut * steps, stride=heads)
        o_all[:, h * hd : (h + 1) * hd] = o_buf[take, :]
        stats = jnp.where(lane == h, m_buf[take, :], stats)
        stats = jnp.where(lane == 24 + h, l_buf[take, :], stats)
    st_all[...] = stats
    if slot != 0:
        msg_ref = refs[0]
        msg_ref[:, : heads * hd] = o_all[...].astype(BF16)
        msg_ref[:, heads * hd :] = pack_stats(st_all[...])


def merged(heads, o_ref, st_ref, recv_refs):
    hd = o_ref.shape[1] // heads
    stats = [st_ref[...]] + [unpack_stats(ref[:, heads * hd :]) for ref in recv_refs]
    top = functools.reduce(jnp.maximum, stats)
    factors = [jnp.exp(one - top) for one in stats]
    total = sum(one * pltpu.roll(factor, 24, 1) for one, factor in zip(stats, factors))
    lane = lane_ids(top.shape[0])
    joint = jnp.where(lane < heads, top, jnp.where((lane >= 24) & (lane < 24 + heads), total, 0.0))

    def head(h):
        cols = slice(h * hd, (h + 1) * hd)
        value = o_ref[:, cols] * factors[0][:, h : h + 1]
        for ref, factor in zip(recv_refs, factors[1:]):
            value += ref[:, cols].astype(F32) * factor[:, h : h + 1]
        return value

    return joint, head


def merge_kernel(heads, o_ref, st_ref, *refs):
    *recv_refs, o_out, st_out, msg_out = refs
    stats, head = merged(heads, o_ref, st_ref, recv_refs)
    hd = o_ref.shape[1] // heads
    for h in range(heads):
        value = head(h)
        o_out[:, h * hd : (h + 1) * hd] = value
        msg_out[:, h * hd : (h + 1) * hd] = value.astype(BF16)
    st_out[...] = stats
    msg_out[:, heads * hd :] = pack_stats(stats)


def finish_kernel(heads, o_ref, st_ref, recv_ref, after_ref, att_ref, done_ref):
    stats, head = merged(heads, o_ref, st_ref, [recv_ref])
    done_ref[...] = after_ref[...]
    hd = o_ref.shape[1] // heads
    for h in range(heads):
        att_ref[:, h * hd : (h + 1) * hd] = (head(h) / stats[:, 24 + h : 25 + h]).astype(BF16)


def store_kernel(column, steps, span, seq_ref, len_ref, *refs):
    slot_refs, (c_ref, after_ref, c_out, done_ref, buf, win, sems) = refs[:4], refs[4:]
    done_ref[...] = after_ref[...]
    requests, rows_kv, hd = c_ref.shape
    window = win.shape[1]
    kv = rows_kv // span
    cut = requests // 4
    fresh = steps * kv
    seq = seq_ref[0]
    whole = pltpu.make_async_copy(c_ref, c_out, sems.at[requests])
    whole.start()
    for g in range(kv):
        at = column + g * hd
        for j, ref in enumerate(slot_refs):
            buf[pl.ds(j * cut * fresh + g, cut * steps, stride=kv), :] = ref[:, at : at + hd].astype(F32)
    line = lax.broadcasted_iota(jnp.int32, (window, hd), 0)
    place = lax.broadcasted_iota(jnp.int32, (window, fresh), 0) - lax.broadcasted_iota(
        jnp.int32, (window, fresh), 1
    )
    pieces = []
    for n in range(requests):
        request = ((seq & 3) ^ (n // cut)) * cut + n % cut
        base = (len_ref[request] - seq * span) * kv
        start = pl.multiple_of(jnp.clip((base // 16) * 16, 0, rows_kv - window), 16)
        touched = (base > -fresh) & (base < rows_kv)
        pieces.append((touched, start, request))

        @pl.when(touched)
        def _():
            pick = jnp.where(place == base - start, 1.0, 0.0).astype(BF16)
            new = (line >= base - start) & (line < base - start + fresh)
            rows = buf[n * fresh : (n + 1) * fresh, :].astype(BF16)
            put = jnp.dot(pick, rows, preferred_element_type=F32)
            old = c_ref[request, pl.ds(start, window), :].astype(F32)
            win[n] = jnp.where(new, put, old).astype(BF16)

    whole.wait()
    for act in ("start", "wait"):
        for n, (touched, start, request) in enumerate(pieces):

            @pl.when(touched)
            def _():
                copy = pltpu.make_async_copy(win.at[n], c_out.at[request, pl.ds(start, window), :], sems.at[n])
                getattr(copy, act)()


def mix_kernel(seq_ref, core_ref, a0_ref, a1_ref, a2_ref, a3_ref, w_ref, done_ref, mine_ref, other_ref, att_buf):
    part = a0_ref.shape[0]
    for j, ref in enumerate((a0_ref, a1_ref, a2_ref, a3_ref)):
        att_buf[pl.ds(pl.multiple_of(((seq_ref[0] & 3) ^ j) * part, 16), part), :] = ref[...]
    product = jnp.dot(att_buf[...], w_ref[...], preferred_element_type=F32)
    half = product.shape[0] // 2
    low = core_ref[0] == 0
    mine_ref[...] = jnp.where(low, product[:half], product[half:])
    other_ref[...] = jnp.where(low, product[half:], product[:half])


def stack_kernel(*refs):
    *in_refs, out_ref = refs
    at = 0
    for ref in in_refs:
        out_ref[at : at + ref.shape[0]] = ref[...]
        at += ref.shape[0]


def relay_kernel(in_ref, after_ref, out_ref):
    del after_ref
    out_ref[...] = in_ref[...]


def sum_kernel(mine_ref, recv_ref, msg_ref):
    msg_ref[...] = (mine_ref[...].astype(F32) + recv_ref[...].astype(F32)).astype(BF16)


def residual_kernel(steps, core_ref, x_ref, gain_ref, mine_ref, recv_ref, mixed_ref, piece_ref):
    rows = mine_ref.shape[0]
    requests = x_ref.shape[0] // steps
    cut = requests // 4
    core = core_ref[0]

    def source(row):
        quarter = row // (rows // 2)
        request = quarter * cut + row % (rows // 2) // steps
        return row % steps * requests + core * (requests // 2) + request

    part = mine_ref[...].astype(F32) + recv_ref[...].astype(F32)
    mixed = reorder(rows, source, x_ref[...]) + part
    mixed_ref[...] = mixed
    squares = jnp.sum(mixed * mixed, axis=1, keepdims=True)
    stats = jnp.where(lane_ids(rows) == 0, squares, 0.0)
    piece_ref[0, :, :LANES] = pack_stats(stats)
    piece_ref[0, :, LANES:] = (mixed * gain_ref[...].astype(F32)).astype(BF16)


def gather_products(masks, seq, own_ref, far_ref, wg_ref, wu_ref, so_far):
    width = own_ref.shape[2] - LANES
    squares = []
    for ref in (own_ref, far_ref):
        squares.append(sum(unpack_stats(ref[j, :, :LANES]) for j in range(len(masks))))
    squares = jnp.concatenate(squares, axis=0)
    gate = up = 0.0
    for j, mask in enumerate(masks):
        take = pl.ds(pl.multiple_of((seq ^ mask) * width, 16), width)
        x = jnp.concatenate([own_ref[j, :, LANES:], far_ref[j, :, LANES:]], axis=0)
        gate += jnp.dot(x, wg_ref[take, :], preferred_element_type=F32)
        up += jnp.dot(x, wu_ref[take, :], preferred_element_type=F32)
    return [new + ref[...] for new, ref in zip((squares, gate, up), so_far)] if so_far else (squares, gate, up)


def products_kernel(masks, seq_ref, own_ref, far_ref, wg_ref, wu_ref, *refs):
    found = gather_products(masks, seq_ref[0], own_ref, far_ref, wg_ref, wu_ref, refs[:-3])
    for ref, value in zip(refs[-3:], found):
        ref[...] = value


def hidden_kernel(masks, features, seq_ref, own_ref, far_ref, wg_ref, wu_ref, sq_ref, gate_ref, up_ref, h_ref):
    squares, gate, up = gather_products(
        masks, seq_ref[0], own_ref, far_ref, wg_ref, wu_ref, (sq_ref, gate_ref, up_ref)
    )
    scale = lax.rsqrt(squares[:, 0:1] / features + 1e-05)
    gate = gate * scale
    up = up * scale
    h_ref[...] = (gate / (1.0 + jnp.exp(-gate)) * up).astype(BF16)


def down_kernel(masks, seq_ref, h_ref, w_ref, *refs):
    own_ref, far_ref = refs[-2:]
    half, width = own_ref.shape[1:]
    hidden = h_ref[...]
    for j, mask in enumerate(masks):
        take = pl.ds(pl.multiple_of((seq_ref[0] ^ mask) * width, LANES), width)
        part = jnp.dot(hidden, w_ref[:, take], preferred_element_type=F32)
        own_ref[j] = part[:half]
        far_ref[j] = part[half:].astype(BF16)


def fold_kernel(acc_ref, *refs):
    *recv_refs, keep_ref, msg_ref = refs
    count = acc_ref.shape[0] // 2
    for j in range(2 * count):
        total = acc_ref[j]
        for ref in recv_refs:
            total += ref[j].astype(F32)
        if j < count:
            keep_ref[j] = total
        else:
            msg_ref[j - count] = total.astype(BF16)


def end_kernel(mixed_ref, mine_ref, recv_ref, out_ref):
    part = mine_ref[0].astype(F32) + recv_ref[0].astype(F32)
    out_ref[...] = (mixed_ref[...] + part).astype(BF16)


def join_kernel(steps, core_ref, own_ref, far_ref, out_ref):
    rows = out_ref.shape[0]
    requests = rows // steps
    cut = requests // 4
    low = core_ref[0] == 0
    own, far = own_ref[...], far_ref[...]
    whole = jnp.concatenate([jnp.where(low, own, far), jnp.where(low, far, own)], axis=0)

    def source(row):
        request = row % requests
        return request * steps + row // requests

    out_ref[...] = reorder(rows, source, whole).astype(BF16)


def per_device(
    n_seq,
    n_tp,
    tokens,
    attn_gain,
    w_query,
    w_key,
    w_value,
    w_out,
    ffn_gain,
    w_gate,
    w_up,
    w_down,
    key_cache,
    value_cache,
    lengths,
):
    steps, requests, width = tokens.shape
    span, kv, hd = key_cache.shape[1:]
    heads = w_query.shape[1] // hd
    cut = requests // 4
    part = steps * cut
    half, rows = 2 * part, 4 * part
    features = width * n_seq
    hidden_width = w_gate.shape[1]
    wide = w_query.shape[1] + w_key.shape[1] + w_value.shape[1] + LANES
    seq = lax.axis_index("seq").astype(jnp.int32)
    core = lax.axis_index("tp").astype(jnp.int32) & 1
    seq_arr, core_arr = seq.reshape(1), core.reshape(1)
    rest = [1 << b for b in range(2, n_seq.bit_length() - 1)]
    tp_bits = [1 << b for b in range(n_tp.bit_length() - 1)]
    masks = [0]
    for bit in reversed(rest):
        masks = masks + [m ^ bit for m in masks]
    slots = [[m ^ j for m in masks] for j in range(4)]

    def hop(value, axis, bit):
        size = n_seq if axis == "seq" else n_tp
        return lax.ppermute(value, axis, [(i, i ^ bit) for i in range(size)])

    x = tokens.reshape(rows, width)
    flat = (requests, span * kv, hd)
    k_flat, v_flat = key_cache.reshape(flat), value_cache.reshape(flat)

    own_lengths = lax.dynamic_slice_in_dim(lengths, (seq & 3) * cut, cut, 0)
    positions = (own_lengths[:, None] + jnp.arange(steps, dtype=jnp.int32)[None, :]).reshape(part)
    freqs = jnp.exp(jnp.arange(hd // 2, dtype=F32) * (-2.0 * math.log(100000000.0) / hd))
    angles = positions.astype(F32)[:, None] * freqs[None, :]
    cosine, sine = jnp.cos(angles), jnp.sin(angles)
    cosine = jnp.concatenate([cosine, cosine], axis=1)
    sine = jnp.concatenate([-sine, sine], axis=1)

    with jax.named_scope("project"):
        sums = [sds((part, wide), F32), sds((part, wide), BF16)]
        acc, *msgs = call(
            functools.partial(project_kernel, steps),
            sums + sums[1:] * 2,
            [SMEM] + [HBM] * 5,
            [
                pltpu.VMEM(x.shape, BF16),
                pltpu.VMEM(attn_gain.shape, BF16),
                pltpu.VMEM(w_query.shape, BF16),
                pltpu.VMEM(w_key.shape, BF16),
                pltpu.VMEM(w_value.shape, BF16),
                pltpu.SemaphoreType.DMA((5,)),
            ],
            limit=60,
        )(seq_arr, x, attn_gain, w_query, w_key, w_value)
        arrived = [hop(msgs[j - 1], "seq", j) for j in (3, 2, 1)]
        (acc,) = call(keep_kernel, sums[:1], [VMEM])(acc)
        for bit in rest:
            acc, msg = call(add_kernel, sums, [VMEM] * (1 + len(arrived)))(acc, *arrived)
            arrived = [hop(msg, "seq", bit)]
        (finished,) = call(
            functools.partial(rotate_kernel, heads, kv, hd, features),
            [sds((part, wide - LANES), BF16)],
            [VMEM] * 4,
        )(acc, arrived[0], cosine, sine)
        found = {j: hop(finished, "seq", j) for j in (3, 2, 1)}
        found[0] = finished

    with jax.named_scope("attend"):
        block = steps * heads
        fresh = steps * kv
        joint = [
            sds((part, heads * hd), F32),
            sds((part, LANES), F32),
            sds((part, heads * hd + LANES), BF16),
        ]
        scratch = [
            pltpu.VMEM((cut * block, hd), F32),
            pltpu.VMEM((cut * fresh, hd), F32),
            pltpu.VMEM((cut * fresh, hd), F32),
            pltpu.VMEM((cut * block, flat[1]), F32),
            pltpu.VMEM((cut * block, hd), F32),
            pltpu.VMEM((cut * block, hd), F32),
            pltpu.VMEM((cut * block, hd), F32),
            pltpu.VMEM((part, heads * hd), F32),
            pltpu.VMEM((part, LANES), F32),
        ]

        def attend(slot):
            return call(
                functools.partial(attend_kernel, heads, kv, steps, span, slot),
                joint[2:] if slot else joint[:2],
                [SMEM, SMEM] + [VMEM] * 3,
                scratch,
                cost=20,
            )(seq_arr, lengths, found[slot], k_flat, v_flat)

        o, st = attend(0)
        arrived = [hop(attend(j)[0], "seq", j) for j in (3, 2, 1)]
        for bit in rest:
            o, st, msg = call(
                functools.partial(merge_kernel, heads), joint, [VMEM] * (2 + len(arrived))
            )(o, st, *arrived)
            arrived = [hop(msg, "seq", bit)]

        def store(column, cache, after):
            return call(
                functools.partial(store_kernel, column * hd, steps, span),
                [sds(flat, BF16), sds((part, LANES), F32)],
                [SMEM, SMEM] + [VMEM] * 6,
                [
                    pltpu.VMEM((requests * fresh, hd), F32),
                    pltpu.VMEM((requests, 16 + -(-fresh // 16) * 16, hd), BF16),
                    pltpu.SemaphoreType.DMA((requests + 1,)),
                ],
                [HBM, VMEM],
            )(seq_arr, lengths, *(found[j] for j in range(4)), cache, after)

        keys, done = store(heads, k_flat, st)
        attended, done = call(
            functools.partial(finish_kernel, heads),
            [sds((part, heads * hd), BF16), sds((part, LANES), F32)],
            [VMEM] * 4,
        )(o, st, arrived[0], done)
        values, done = store(heads + kv, v_flat, done)
        found = {j: hop(attended, "seq", j) for j in (3, 2, 1)}
        found[0] = attended

    with jax.named_scope("mix"):
        mine, other = call(
            mix_kernel,
            [sds((half, width), F32)] * 2,
            [SMEM, SMEM] + [VMEM] * 6,
            [pltpu.VMEM((rows, heads * hd), BF16)],
        )(seq_arr, core_arr, *(found[j] for j in range(4)), w_out, done)
        summed = mine, hop(other, "tp", 1)
        for bit in tp_bits[1:]:
            (msg,) = call(sum_kernel, [sds((half, width), BF16)], [VMEM] * 2)(*summed)
            summed = msg, hop(msg, "tp", bit)
        gain = lax.dynamic_slice_in_dim(ffn_gain, seq * width, width, 0).reshape(1, width)
        mixed, pieces = call(
            functools.partial(residual_kernel, steps),
            [sds((half, width), F32), sds((1, half, LANES + width), BF16)],
            [SMEM] + [VMEM] * 4,
            cost=6,
        )(core_arr, x, gain, *summed)
        for bit in reversed(rest):
            (pieces,) = call(
                stack_kernel,
                [sds((2 * pieces.shape[0],) + pieces.shape[1:], BF16)],
                [VMEM] * 2,
                cost=8,
            )(pieces, hop(pieces, "seq", bit))

    with jax.named_scope("ffn"):
        found = {j: hop(pieces, "seq", j) for j in (3, 2, 1)}
        found[0] = pieces
        order = (0, 3, 2, 1)
        state = []
        earlier = []
        for n, j in enumerate(order):
            piece = found[j]
            if n:
                (piece,) = call(relay_kernel, [sds(piece.shape, BF16)], [VMEM] * 2, cost=1)(
                    piece, earlier[max(n - 2, 0)]
                )
            last = n == 3
            state = call(
                functools.partial(hidden_kernel, slots[j], features)
                if last
                else functools.partial(products_kernel, slots[j]),
                [sds((rows, hidden_width), BF16)]
                if last
                else [sds((rows, LANES), F32)] + [sds((rows, hidden_width), F32)] * 2,
                [SMEM] + [VMEM] * (4 + len(state)),
                cost=1,
            )(seq_arr, found[j], hop(piece, "tp", 1), w_gate, w_up, *state)
            earlier.append(state[0])
        (hidden,) = state

        shape = (len(masks), half, width)

        def down(some, *after):
            if width % LANES == 0:
                return call(
                    functools.partial(down_kernel, some),
                    [sds(shape, F32), sds(shape, BF16)],
                    [SMEM] + [VMEM] * (2 + len(after)),
                    cost=1,
                )(seq_arr, hidden, w_down, *after)
            whole = jnp.dot(hidden, w_down, preferred_element_type=F32)
            whole = whole.reshape(rows, n_seq, width).transpose(1, 0, 2)
            whole = jnp.take(whole, seq ^ jnp.array(some, jnp.int32), axis=0)
            return whole[:, :half], whole[:, half:].astype(BF16)

        arrived = []
        for j in (3, 2, 1):
            own, far = down(slots[j])
            (msg,) = call(sum_kernel, [sds(shape, BF16)], [VMEM] * 2)(own, hop(far, "tp", 1))
            arrived.append(hop(msg, "seq", j))
        keep, far = down(slots[0], msg)
        arrived.append(hop(far, "tp", 1))
        for bit in rest:
            shape = (keep.shape[0] // 2, half, width)
            keep, msg = call(fold_kernel, [sds(shape, F32), sds(shape, BF16)], [VMEM] * (1 + len(arrived)))(
                keep, *arrived
            )
            arrived = [hop(msg, "seq", bit)]
        shape = (1, half, width)
        summed = keep, arrived[0]
        for bit in tp_bits[1:]:
            (msg,) = call(sum_kernel, [sds(shape, BF16)], [VMEM] * 2)(*summed)
            summed = msg, hop(msg, "tp", bit)
        (own,) = call(end_kernel, [sds((half, width), BF16)], [VMEM] * 3)(mixed, *summed)
        (result,) = call(functools.partial(join_kernel, steps), [sds(x.shape, BF16)], [SMEM] + [VMEM] * 2)(
            core_arr, own, hop(own, "tp", 1)
        )
    return result.reshape(tokens.shape), keys.reshape(key_cache.shape), values.reshape(value_cache.shape)


def solution(mesh):
    placed = (
        P(None, None, "seq"),
        P("seq"),
        P("seq", "tp"),
        P("seq", "tp"),
        P("seq", "tp"),
        P("tp", "seq"),
        P(),
        P(None, ("seq", "tp")),
        P(None, ("seq", "tp")),
        P(("seq", "tp"), None),
        P(None, "seq", "tp", None),
        P(None, "seq", "tp", None),
        P(),
    )
    return jax.shard_map(
        functools.partial(per_device, mesh.shape["seq"], mesh.shape["tp"]),
        mesh=mesh,
        in_specs=placed,
        out_specs=(P(None, None, "seq"), P(None, "seq", "tp", None), P(None, "seq", "tp", None)),
        check_vma=False,
    )
```

```python
import functools
import math

import jax
import jax.numpy as jnp
from jax import lax
from jax.experimental import pallas as pl
from jax.experimental.pallas import tpu as pltpu
from jax.sharding import PartitionSpec as P

F32 = jnp.float32
BF16 = jnp.bfloat16
LANES = 128
VMEM = pl.BlockSpec(memory_space=pltpu.VMEM)
SMEM = pl.BlockSpec(memory_space=pltpu.SMEM)
HBM = pl.BlockSpec(memory_space=pltpu.HBM)


def call(body, outs, ins, scratch=(), places=None, cost=3, limit=8):
    return pl.pallas_call(
        body,
        out_shape=outs,
        in_specs=ins,
        out_specs=places or [VMEM] * len(outs),
        scratch_shapes=list(scratch),
        cost_estimate=pl.CostEstimate(flops=int(cost * 1.15e9), bytes_accessed=1 << 20, transcendentals=0),
        compiler_params=pltpu.CompilerParams(vmem_limit_bytes=int(limit * 2**20)),
    )


def sds(shape, dtype):
    return jax.ShapeDtypeStruct(shape, dtype)


def lane_ids(rows):
    return lax.broadcasted_iota(jnp.int32, (rows, LANES), 1)


def split3(value):
    high = value.astype(BF16)
    rest = value - high.astype(F32)
    mid = rest.astype(BF16)
    low = (rest - mid.astype(F32)).astype(BF16)
    return high, mid, low


def pack_stats(stats):
    high, mid, low = (part.astype(F32) for part in split3(stats))
    return (high + pltpu.roll(mid, 8, 1) + pltpu.roll(low, 16, 1)).astype(BF16)


def unpack_stats(packed):
    packed = packed.astype(F32)
    return (packed + pltpu.roll(packed, LANES - 8, 1)) + pltpu.roll(packed, LANES - 16, 1)


def reorder(rows, source, x):
    shape = (rows, x.shape[0])
    row = lax.broadcasted_iota(jnp.int32, shape, 0)
    col = lax.broadcasted_iota(jnp.int32, shape, 1)
    pick = jnp.where(col == source(row), 1.0, 0.0).astype(BF16)
    return jnp.dot(pick, x, preferred_element_type=F32)


def project_kernel(
    steps,
    seq_ref,
    x_hbm,
    gain_hbm,
    wq_hbm,
    wk_hbm,
    wv_hbm,
    acc_ref,
    msg1_ref,
    msg2_ref,
    msg3_ref,
    x_ref,
    gain_ref,
    wq_ref,
    wk_ref,
    wv_ref,
    sems,
):
    copies = [
        pltpu.make_async_copy(source, target, sems.at[i])
        for i, (source, target) in enumerate(
            (
                (x_hbm, x_ref),
                (gain_hbm, gain_ref),
                (wq_hbm, wq_ref),
                (wk_hbm, wk_ref),
                (wv_hbm, wv_ref),
            )
        )
    ]
    for copy in copies:
        copy.start()
    copies[0].wait()
    copies[1].wait()
    rows = x_ref.shape[0]
    requests = rows // steps
    cut = requests // 4
    part = rows // 4
    place = seq_ref[0] & 3

    def source(row):
        return row % steps * requests + ((row // part) ^ place) * cut + row % part // steps

    x = reorder(rows, source, x_ref[...])
    normed = (x * gain_ref[...].astype(F32)).astype(BF16)
    squares = jnp.sum(x * x, axis=1, keepdims=True)
    msgs = (msg1_ref, msg2_ref, msg3_ref)
    at = 0
    for copy, w_ref in zip(copies[2:], (wq_ref, wk_ref, wv_ref)):
        copy.wait()
        width = w_ref.shape[1]
        product = jnp.dot(normed, w_ref[...], preferred_element_type=F32)
        acc_ref[:, at : at + width] = product[:part]
        for j, ref in enumerate(msgs):
            ref[:, at : at + width] = product[(j + 1) * part : (j + 2) * part].astype(BF16)
        at += width
    stats = jnp.where(lane_ids(rows) == 0, squares, 0.0)
    acc_ref[:, at:] = stats[:part]
    packed = pack_stats(stats)
    for j, ref in enumerate(msgs):
        ref[:, at:] = packed[(j + 1) * part : (j + 2) * part]


def keep_kernel(in_ref, out_ref):
    out_ref[...] = in_ref[...]


def add_kernel(acc_ref, *refs):
    *recv_refs, out_ref, msg_ref = refs
    at = acc_ref.shape[1] - LANES
    total, stats = acc_ref[:, :at], acc_ref[:, at:]
    for ref in recv_refs:
        total += ref[:, :at].astype(F32)
        stats += unpack_stats(ref[:, at:])
    stats = jnp.where(lane_ids(stats.shape[0]) == 0, stats, 0.0)
    out_ref[:, :at] = total
    msg_ref[:, :at] = total.astype(BF16)
    out_ref[:, at:] = stats
    msg_ref[:, at:] = pack_stats(stats)


def rotate_kernel(heads, kv, hd, features, acc_ref, recv_ref, cos_ref, sin_ref, out_ref):
    at = (heads + 2 * kv) * hd
    squares = acc_ref[:, at:] + unpack_stats(recv_ref[:, at:])
    scale = lax.rsqrt(squares[:, 0:1] / features + 1e-05)
    for index in range(heads + 2 * kv):
        cols = slice(index * hd, (index + 1) * hd)
        value = (acc_ref[:, cols] + recv_ref[:, cols].astype(F32)) * scale
        if index < heads + kv:
            value = value * cos_ref[...] + pltpu.roll(value, hd // 2, 1) * sin_ref[...]
        out_ref[:, cols] = value.astype(BF16)


def attend_kernel(heads, kv, steps, span, slots, seq_ref, len_ref, *refs):
    rows_refs, refs = refs[: len(slots)], refs[len(slots) :]
    k_ref, v_ref, *outs = refs[:-7]
    q_buf, kn_buf, vn_buf, s_buf, o_buf, m_buf, l_buf = refs[-7:]
    requests, rows_kv, hd = k_ref.shape
    cut = requests // 4
    part = cut * steps
    group = heads // kv
    block = steps * heads
    fresh = steps * kv
    seq = seq_ref[0]
    first = seq * span
    taken = [((seq & 3) ^ slot) * cut + r for slot in slots for r in range(cut)]

    for n, rows_ref in enumerate(rows_refs):

        def spread(buf, index, place, per_row):
            value = rows_ref[:, index * hd : (index + 1) * hd].astype(F32)
            buf[pl.ds(n * part * per_row + place, part, stride=per_row), :] = value

        for h in range(heads):
            spread(q_buf, h, h, heads)
        for g in range(kv):
            spread(kn_buf, heads + g, g, kv)
            spread(vn_buf, heads + kv + g, g, kv)
    shrink = hd ** (-0.5)
    queries = q_buf[...].astype(BF16)

    row = lax.broadcasted_iota(jnp.int32, (block, rows_kv), 0)
    col = lax.broadcasted_iota(jnp.int32, (block, rows_kv), 1)
    need = jnp.where((row % heads) // group == col % kv, col // kv, 1 << 29)
    for r, request in enumerate(taken):
        scores = lax.dot_general(
            queries[r * block : (r + 1) * block],
            k_ref[request],
            (((1,), (1,)), ((), ())),
            preferred_element_type=F32,
        )
        live = need < len_ref[request] - first
        s_buf[r * block : (r + 1) * block, :] = jnp.where(live, scores * shrink, -1e30)

    k_new = kn_buf[...].astype(BF16)
    v_new = vn_buf[...].astype(BF16)
    shape = (len(taken) * block, len(taken) * fresh)
    row = lax.broadcasted_iota(jnp.int32, shape, 0)
    col = lax.broadcasted_iota(jnp.int32, shape, 1)
    col_row = lax.broadcasted_iota(jnp.int32, (1, shape[1]), 1)
    at_position = (col_row % fresh) // kv - first
    for r, request in enumerate(taken):
        at_position += jnp.where(col_row // fresh == r, len_ref[request], 0)
    held = (at_position >= 0) & (at_position < span)
    new_live = (
        (row // block == col // fresh)
        & ((row % heads) // group == col % kv)
        & ((row % block) // heads >= (col % fresh) // kv)
        & held
    )
    new_scores = lax.dot_general(queries, k_new, (((1,), (1,)), ((), ())), preferred_element_type=F32)
    new_scores = jnp.where(new_live, new_scores * shrink, -1e30)

    scores = s_buf[...]
    top = jnp.maximum(jnp.max(scores, axis=1, keepdims=True), jnp.max(new_scores, axis=1, keepdims=True))
    top = jnp.maximum(top, -1e29)
    expo = jnp.exp(scores - top)
    new_expo = jnp.exp(new_scores - top)
    total = jnp.sum(expo, axis=1, keepdims=True) + jnp.sum(new_expo, axis=1, keepdims=True)
    m_buf[...] = jnp.broadcast_to(top, m_buf.shape)
    l_buf[...] = jnp.broadcast_to(total, l_buf.shape)
    expo = expo.astype(BF16)
    new_part = jnp.dot(new_expo.astype(BF16), v_new, preferred_element_type=F32)
    for r, request in enumerate(taken):
        mine = slice(r * block, (r + 1) * block)
        o_buf[mine, :] = new_part[mine] + jnp.dot(expo[mine], v_ref[request], preferred_element_type=F32)

    lane = lane_ids(part)
    for n, slot in enumerate(slots):
        stats = jnp.zeros((part, LANES), F32)
        for h in range(heads):
            take = pl.ds(n * part * heads + h, part, stride=heads)
            value = o_buf[take, :]
            cols = slice(h * hd, (h + 1) * hd)
            if slot:
                outs[n][:, cols] = value.astype(BF16)
            else:
                outs[0][:, cols] = value
            stats = jnp.where(lane == h, m_buf[take, :], stats)
            stats = jnp.where(lane == 24 + h, l_buf[take, :], stats)
        if slot:
            outs[n][:, heads * hd :] = pack_stats(stats)
        else:
            outs[1][...] = stats


def merged(heads, o_ref, st_ref, recv_refs):
    hd = o_ref.shape[1] // heads
    stats = [st_ref[...]] + [unpack_stats(ref[:, heads * hd :]) for ref in recv_refs]
    top = functools.reduce(jnp.maximum, stats)
    factors = [jnp.exp(one - top) for one in stats]
    total = sum(one * pltpu.roll(factor, 24, 1) for one, factor in zip(stats, factors))
    lane = lane_ids(top.shape[0])
    joint = jnp.where(lane < heads, top, jnp.where((lane >= 24) & (lane < 24 + heads), total, 0.0))

    def head(h):
        cols = slice(h * hd, (h + 1) * hd)
        value = o_ref[:, cols] * factors[0][:, h : h + 1]
        for ref, factor in zip(recv_refs, factors[1:]):
            value += ref[:, cols].astype(F32) * factor[:, h : h + 1]
        return value

    return joint, head


def merge_kernel(heads, o_ref, st_ref, *refs):
    *recv_refs, o_out, st_out, msg_out = refs
    stats, head = merged(heads, o_ref, st_ref, recv_refs)
    hd = o_ref.shape[1] // heads
    for h in range(heads):
        value = head(h)
        o_out[:, h * hd : (h + 1) * hd] = value
        msg_out[:, h * hd : (h + 1) * hd] = value.astype(BF16)
    st_out[...] = stats
    msg_out[:, heads * hd :] = pack_stats(stats)


def finish_kernel(heads, o_ref, st_ref, recv_ref, after_ref, att_ref, done_ref):
    stats, head = merged(heads, o_ref, st_ref, [recv_ref])
    done_ref[...] = after_ref[...]
    hd = o_ref.shape[1] // heads
    for h in range(heads):
        att_ref[:, h * hd : (h + 1) * hd] = (head(h) / stats[:, 24 + h : 25 + h]).astype(BF16)


def store_kernel(column, steps, span, seq_ref, len_ref, *refs):
    slot_refs, (c_ref, after_ref, c_out, done_ref, buf, win, sems) = refs[:4], refs[4:]
    done_ref[...] = after_ref[...]
    requests, rows_kv, hd = c_ref.shape
    window = win.shape[1]
    kv = rows_kv // span
    cut = requests // 4
    fresh = steps * kv
    seq = seq_ref[0]
    whole = pltpu.make_async_copy(c_ref, c_out, sems.at[requests])
    whole.start()
    for g in range(kv):
        at = column + g * hd
        for j, ref in enumerate(slot_refs):
            buf[pl.ds(j * cut * fresh + g, cut * steps, stride=kv), :] = ref[:, at : at + hd].astype(F32)
    line = lax.broadcasted_iota(jnp.int32, (window, hd), 0)
    place = lax.broadcasted_iota(jnp.int32, (window, fresh), 0) - lax.broadcasted_iota(
        jnp.int32, (window, fresh), 1
    )
    pieces = []
    for n in range(requests):
        request = ((seq & 3) ^ (n // cut)) * cut + n % cut
        base = (len_ref[request] - seq * span) * kv
        start = pl.multiple_of(jnp.clip((base // 16) * 16, 0, rows_kv - window), 16)
        touched = (base > -fresh) & (base < rows_kv)
        pieces.append((touched, start, request))

        @pl.when(touched)
        def _():
            pick = jnp.where(place == base - start, 1.0, 0.0).astype(BF16)
            new = (line >= base - start) & (line < base - start + fresh)
            rows = buf[n * fresh : (n + 1) * fresh, :].astype(BF16)
            put = jnp.dot(pick, rows, preferred_element_type=F32)
            old = c_ref[request, pl.ds(start, window), :].astype(F32)
            win[n] = jnp.where(new, put, old).astype(BF16)

    whole.wait()
    for act in ("start", "wait"):
        for n, (touched, start, request) in enumerate(pieces):

            @pl.when(touched)
            def _():
                copy = pltpu.make_async_copy(win.at[n], c_out.at[request, pl.ds(start, window), :], sems.at[n])
                getattr(copy, act)()


def mix_kernel(seq_ref, core_ref, a0_ref, a1_ref, a2_ref, a3_ref, w_ref, done_ref, mine_ref, other_ref, att_buf):
    part = a0_ref.shape[0]
    for j, ref in enumerate((a0_ref, a1_ref, a2_ref, a3_ref)):
        att_buf[pl.ds(pl.multiple_of(((seq_ref[0] & 3) ^ j) * part, 16), part), :] = ref[...]
    product = jnp.dot(att_buf[...], w_ref[...], preferred_element_type=F32)
    half = product.shape[0] // 2
    low = core_ref[0] == 0
    mine_ref[...] = jnp.where(low, product[:half], product[half:])
    other_ref[...] = jnp.where(low, product[half:], product[:half])


def stack_kernel(*refs):
    *in_refs, out_ref = refs
    at = 0
    for ref in in_refs:
        out_ref[at : at + ref.shape[0]] = ref[...]
        at += ref.shape[0]


def relay_kernel(in_ref, after_ref, out_ref):
    del after_ref
    out_ref[...] = in_ref[...]


def sum_kernel(mine_ref, recv_ref, *msg_refs):
    count = mine_ref.shape[0] // len(msg_refs)
    for i, ref in enumerate(msg_refs):
        some = slice(i * count, (i + 1) * count)
        ref[...] = (mine_ref[some].astype(F32) + recv_ref[some].astype(F32)).astype(BF16)


def residual_kernel(steps, core_ref, x_ref, gain_ref, mine_ref, recv_ref, mixed_ref, piece_ref):
    rows = mine_ref.shape[0]
    requests = x_ref.shape[0] // steps
    cut = requests // 4
    core = core_ref[0]

    def source(row):
        quarter = row // (rows // 2)
        request = quarter * cut + row % (rows // 2) // steps
        return row % steps * requests + core * (requests // 2) + request

    part = mine_ref[...].astype(F32) + recv_ref[...].astype(F32)
    mixed = reorder(rows, source, x_ref[...]) + part
    mixed_ref[...] = mixed
    squares = jnp.sum(mixed * mixed, axis=1, keepdims=True)
    stats = jnp.where(lane_ids(rows) == 0, squares, 0.0)
    piece_ref[0, :, :LANES] = pack_stats(stats)
    piece_ref[0, :, LANES:] = (mixed * gain_ref[...].astype(F32)).astype(BF16)


def gather_products(masks, seq, own_ref, far_ref, wg_ref, wu_ref, so_far):
    width = own_ref.shape[2] - LANES
    squares = []
    for ref in (own_ref, far_ref):
        squares.append(sum(unpack_stats(ref[j, :, :LANES]) for j in range(len(masks))))
    squares = jnp.concatenate(squares, axis=0)
    gate = up = 0.0
    for j, mask in enumerate(masks):
        take = pl.ds(pl.multiple_of((seq ^ mask) * width, 16), width)
        x = jnp.concatenate([own_ref[j, :, LANES:], far_ref[j, :, LANES:]], axis=0)
        gate += jnp.dot(x, wg_ref[take, :], preferred_element_type=F32)
        up += jnp.dot(x, wu_ref[take, :], preferred_element_type=F32)
    return [new + ref[...] for new, ref in zip((squares, gate, up), so_far)] if so_far else (squares, gate, up)


def products_kernel(masks, features, taken, seq_ref, own_ref, far_ref, wg_ref, wu_ref, *refs):
    copies = []
    if taken:
        w_hbm, *refs = refs
        refs, w_refs, sems = refs[: -len(taken) - 1], refs[-len(taken) - 1 : -1], refs[-1]
        for i, (some, w_ref) in enumerate(zip(taken, w_refs)):
            width = w_ref.shape[2]
            for j, mask in enumerate(some):
                at = pl.multiple_of((seq_ref[0] ^ mask) * width, LANES)
                copies.append(pltpu.make_async_copy(w_hbm.at[:, pl.ds(at, width)], w_ref.at[j], sems.at[i, j]))
                copies[-1].start()
    outs = refs[-1:] if features else refs[-3:]
    found = gather_products(masks, seq_ref[0], own_ref, far_ref, wg_ref, wu_ref, refs[: -len(outs)])
    if features:
        found = [hidden_units(features, *found)]
    for ref, value in zip(outs, found):
        ref[...] = value
    for copy in copies:
        copy.wait()


def hidden_units(features, squares, gate, up):
    scale = lax.rsqrt(squares[:, 0:1] / features + 1e-05)
    gate = gate * scale
    up = up * scale
    return (gate / (1.0 + jnp.exp(-gate)) * up).astype(BF16)


def down_kernel(count, h_ref, *refs):
    own_ref, far_ref = refs[-2:]
    half = own_ref.shape[1]
    hidden = h_ref[...]
    at = 0
    for w_ref in refs[:count]:
        for j in range(w_ref.shape[0]):
            part = jnp.dot(hidden, w_ref[j], preferred_element_type=F32)
            own_ref[at + j] = part[:half]
            far_ref[at + j] = part[half:].astype(BF16)
        at += w_ref.shape[0]


def fold_kernel(acc_ref, *refs):
    *recv_refs, keep_ref, msg_ref = refs
    count = acc_ref.shape[0] // 2
    for j in range(2 * count):
        total = acc_ref[j]
        for ref in recv_refs:
            total += ref[j].astype(F32)
        if j < count:
            keep_ref[j] = total
        else:
            msg_ref[j - count] = total.astype(BF16)


def end_kernel(mixed_ref, mine_ref, recv_ref, out_ref):
    part = mine_ref[0].astype(F32) + recv_ref[0].astype(F32)
    out_ref[...] = (mixed_ref[...] + part).astype(BF16)


def join_kernel(steps, core_ref, own_ref, far_ref, out_ref):
    rows = out_ref.shape[0]
    requests = rows // steps
    cut = requests // 4
    low = core_ref[0] == 0
    own, far = own_ref[...], far_ref[...]
    whole = jnp.concatenate([jnp.where(low, own, far), jnp.where(low, far, own)], axis=0)

    def source(row):
        request = row % requests
        return request * steps + row // requests

    out_ref[...] = reorder(rows, source, whole).astype(BF16)


def per_device(
    n_seq,
    n_tp,
    tokens,
    attn_gain,
    w_query,
    w_key,
    w_value,
    w_out,
    ffn_gain,
    w_gate,
    w_up,
    w_down,
    key_cache,
    value_cache,
    lengths,
):
    steps, requests, width = tokens.shape
    span, kv, hd = key_cache.shape[1:]
    heads = w_query.shape[1] // hd
    cut = requests // 4
    part = steps * cut
    half, rows = 2 * part, 4 * part
    features = width * n_seq
    hidden_width = w_gate.shape[1]
    wide = w_query.shape[1] + w_key.shape[1] + w_value.shape[1] + LANES
    seq = lax.axis_index("seq").astype(jnp.int32)
    core = lax.axis_index("tp").astype(jnp.int32) & 1
    seq_arr, core_arr = seq.reshape(1), core.reshape(1)
    rest = [1 << b for b in range(2, n_seq.bit_length() - 1)]
    tp_bits = [1 << b for b in range(n_tp.bit_length() - 1)]
    masks = [0]
    for bit in reversed(rest):
        masks = masks + [m ^ bit for m in masks]
    slots = [[m ^ j for m in masks] for j in range(4)]

    def hop(value, axis, bit):
        size = n_seq if axis == "seq" else n_tp
        return lax.ppermute(value, axis, [(i, i ^ bit) for i in range(size)])

    x = tokens.reshape(rows, width)
    flat = (requests, span * kv, hd)
    k_flat, v_flat = key_cache.reshape(flat), value_cache.reshape(flat)

    own_lengths = lax.dynamic_slice_in_dim(lengths, (seq & 3) * cut, cut, 0)
    positions = (own_lengths[:, None] + jnp.arange(steps, dtype=jnp.int32)[None, :]).reshape(part)
    freqs = jnp.exp(jnp.arange(hd // 2, dtype=F32) * (-2.0 * math.log(100000000.0) / hd))
    angles = positions.astype(F32)[:, None] * freqs[None, :]
    cosine, sine = jnp.cos(angles), jnp.sin(angles)
    cosine = jnp.concatenate([cosine, cosine], axis=1)
    sine = jnp.concatenate([-sine, sine], axis=1)

    with jax.named_scope("project"):
        sums = [sds((part, wide), F32), sds((part, wide), BF16)]
        acc, *msgs = call(
            functools.partial(project_kernel, steps),
            sums + sums[1:] * 2,
            [SMEM] + [HBM] * 5,
            [
                pltpu.VMEM(x.shape, BF16),
                pltpu.VMEM(attn_gain.shape, BF16),
                pltpu.VMEM(w_query.shape, BF16),
                pltpu.VMEM(w_key.shape, BF16),
                pltpu.VMEM(w_value.shape, BF16),
                pltpu.SemaphoreType.DMA((5,)),
            ],
            limit=60,
        )(seq_arr, x, attn_gain, w_query, w_key, w_value)
        arrived = [hop(msgs[j - 1], "seq", j) for j in (3, 2, 1)]
        (acc,) = call(keep_kernel, sums[:1], [VMEM])(acc)
        for bit in rest:
            acc, msg = call(add_kernel, sums, [VMEM] * (1 + len(arrived)))(acc, *arrived)
            arrived = [hop(msg, "seq", bit)]
        (finished,) = call(
            functools.partial(rotate_kernel, heads, kv, hd, features),
            [sds((part, wide - LANES), BF16)],
            [VMEM] * 4,
        )(acc, arrived[0], cosine, sine)
        found = {j: hop(finished, "seq", j) for j in (3, 2, 1)}
        found[0] = finished

    with jax.named_scope("attend"):
        block = steps * heads
        fresh = steps * kv
        joint = [
            sds((part, heads * hd), F32),
            sds((part, LANES), F32),
            sds((part, heads * hd + LANES), BF16),
        ]
        def attend(*some):
            count = len(some) * cut
            return call(
                functools.partial(attend_kernel, heads, kv, steps, span, some),
                joint[2:] * len(some) if some[0] else joint[:2],
                [SMEM, SMEM] + [VMEM] * (len(some) + 2),
                [
                    pltpu.VMEM((count * block, hd), F32),
                    pltpu.VMEM((count * fresh, hd), F32),
                    pltpu.VMEM((count * fresh, hd), F32),
                    pltpu.VMEM((count * block, flat[1]), F32),
                    pltpu.VMEM((count * block, hd), F32),
                    pltpu.VMEM((count * block, hd), F32),
                    pltpu.VMEM((count * block, hd), F32),
                ],
                cost=20,
            )(seq_arr, lengths, *(found[j] for j in some), k_flat, v_flat)

        o, st = attend(0)
        arrived = [hop(msg, "seq", j) for some in ((3,), (1, 2)) for j, msg in zip(some, attend(*some))]
        for bit in rest:
            o, st, msg = call(
                functools.partial(merge_kernel, heads), joint, [VMEM] * (2 + len(arrived))
            )(o, st, *arrived)
            arrived = [hop(msg, "seq", bit)]

        def store(column, cache, after):
            return call(
                functools.partial(store_kernel, column * hd, steps, span),
                [sds(flat, BF16), sds((part, LANES), F32)],
                [SMEM, SMEM] + [VMEM] * 6,
                [
                    pltpu.VMEM((requests * fresh, hd), F32),
                    pltpu.VMEM((requests, 16 + -(-fresh // 16) * 16, hd), BF16),
                    pltpu.SemaphoreType.DMA((requests + 1,)),
                ],
                [HBM, VMEM],
            )(seq_arr, lengths, *(found[j] for j in range(4)), cache, after)

        keys, done = store(heads, k_flat, st)
        attended, done = call(
            functools.partial(finish_kernel, heads),
            [sds((part, heads * hd), BF16), sds((part, LANES), F32)],
            [VMEM] * 4,
        )(o, st, arrived[0], done)
        values, done = store(heads + kv, v_flat, done)
        found = {j: hop(attended, "seq", j) for j in (3, 2, 1)}
        found[0] = attended

    with jax.named_scope("mix"):
        mine, other = call(
            mix_kernel,
            [sds((half, width), F32)] * 2,
            [SMEM, SMEM] + [VMEM] * 6,
            [pltpu.VMEM((rows, heads * hd), BF16)],
        )(seq_arr, core_arr, *(found[j] for j in range(4)), w_out, done)
        summed = mine, hop(other, "tp", 1)
        for bit in tp_bits[1:]:
            (msg,) = call(sum_kernel, [sds((half, width), BF16)], [VMEM] * 2)(*summed)
            summed = msg, hop(msg, "tp", bit)
        gain = lax.dynamic_slice_in_dim(ffn_gain, seq * width, width, 0).reshape(1, width)
        mixed, pieces = call(
            functools.partial(residual_kernel, steps),
            [sds((half, width), F32), sds((1, half, LANES + width), BF16)],
            [SMEM] + [VMEM] * 4,
            cost=6,
        )(core_arr, x, gain, *summed)
        for bit in reversed(rest):
            (pieces,) = call(
                stack_kernel,
                [sds((2 * pieces.shape[0],) + pieces.shape[1:], BF16)],
                [VMEM] * 2,
                cost=8,
            )(pieces, hop(pieces, "seq", bit))

    with jax.named_scope("ffn"):
        found = {j: hop(pieces, "seq", j) for j in (3, 2, 1)}
        found[0] = pieces
        order = (0, 3, 2, 1)
        reads = ((3,), (2,), (1,), (0,))
        state = []
        earlier = []
        quarter = {}
        for n, j in enumerate(order):
            piece = found[j]
            if n:
                (piece,) = call(relay_kernel, [sds(piece.shape, BF16)], [VMEM] * 2, cost=1)(
                    piece, earlier[max(n - 2, 0)]
                )
            taken = reads[n] if width % LANES == 0 else ()
            state = call(
                functools.partial(
                    products_kernel, slots[j], features if n == 3 else 0, [slots[i] for i in taken]
                ),
                (
                    [sds((rows, hidden_width), BF16)]
                    if n == 3
                    else [sds((rows, LANES), F32)] + [sds((rows, hidden_width), F32)] * 2
                )
                + [sds((len(masks), hidden_width, width), BF16)] * len(taken),
                [SMEM] + [VMEM] * 4 + [HBM] * (len(taken) > 0) + [VMEM] * len(state),
                [pltpu.SemaphoreType.DMA((len(taken), len(masks)))] * (len(taken) > 0),
                cost=1,
            )(seq_arr, found[j], hop(piece, "tp", 1), w_gate, w_up, *[w_down] * (len(taken) > 0), *state)
            if taken:
                quarter.update(zip(taken, state[-len(taken) :]))
                state = state[: -len(taken)]
            earlier.append(state[0])
        (hidden,) = state

        def down(some, *after):
            shape = (len(some) * len(masks), half, width)
            if quarter:
                return call(
                    functools.partial(down_kernel, len(some)),
                    [sds(shape, F32), sds(shape, BF16)],
                    [VMEM] * (1 + len(some) + len(after)),
                    cost=1,
                )(hidden, *(quarter[j] for j in some), *after)
            whole = jnp.dot(hidden, w_down, preferred_element_type=F32)
            whole = whole.reshape(rows, n_seq, width).transpose(1, 0, 2)
            places = [m for j in some for m in slots[j]]
            whole = jnp.take(whole, seq ^ jnp.array(places, jnp.int32), axis=0)
            return whole[:, :half], whole[:, half:].astype(BF16)

        shape = (len(masks), half, width)
        arrived = []
        sent = []
        after = []
        for some in ((3,), (1, 2)):
            own, far = down(some, *after)
            after = [far]
            msgs = call(sum_kernel, [sds(shape, BF16)] * len(some), [VMEM] * 2)(own, hop(far, "tp", 1))
            sent += msgs
            arrived += [hop(msg, "seq", j) for j, msg in zip(some, msgs)]
        keep, far = down((0,), *sent)
        arrived.append(hop(far, "tp", 1))
        for bit in rest:
            shape = (keep.shape[0] // 2, half, width)
            keep, msg = call(fold_kernel, [sds(shape, F32), sds(shape, BF16)], [VMEM] * (1 + len(arrived)))(
                keep, *arrived
            )
            arrived = [hop(msg, "seq", bit)]
        shape = (1, half, width)
        summed = keep, arrived[0]
        for bit in tp_bits[1:]:
            (msg,) = call(sum_kernel, [sds(shape, BF16)], [VMEM] * 2)(*summed)
            summed = msg, hop(msg, "tp", bit)
        (own,) = call(end_kernel, [sds((half, width), BF16)], [VMEM] * 3)(mixed, *summed)
        (result,) = call(functools.partial(join_kernel, steps), [sds(x.shape, BF16)], [SMEM] + [VMEM] * 2)(
            core_arr, own, hop(own, "tp", 1)
        )
    return result.reshape(tokens.shape), keys.reshape(key_cache.shape), values.reshape(value_cache.shape)


def solution(mesh):
    placed = (
        P(None, None, "seq"),
        P("seq"),
        P("seq", "tp"),
        P("seq", "tp"),
        P("seq", "tp"),
        P("tp", "seq"),
        P(),
        P(None, ("seq", "tp")),
        P(None, ("seq", "tp")),
        P(("seq", "tp"), None),
        P(None, "seq", "tp", None),
        P(None, "seq", "tp", None),
        P(),
    )
    return jax.shard_map(
        functools.partial(per_device, mesh.shape["seq"], mesh.shape["tp"]),
        mesh=mesh,
        in_specs=placed,
        out_specs=(P(None, None, "seq"), P(None, "seq", "tp", None), P(None, "seq", "tp", None)),
        check_vma=False,
    )
```

```python
import functools
import math

import jax
import jax.numpy as jnp
from jax import lax
from jax.experimental import pallas as pl
from jax.experimental.pallas import tpu as pltpu
from jax.sharding import PartitionSpec as P

F32 = jnp.float32
BF16 = jnp.bfloat16
LANES = 128
VMEM = pl.BlockSpec(memory_space=pltpu.VMEM)
SMEM = pl.BlockSpec(memory_space=pltpu.SMEM)
HBM = pl.BlockSpec(memory_space=pltpu.HBM)


def call(body, outs, ins, scratch=(), places=None, cost=3, limit=8):
    return pl.pallas_call(
        body,
        out_shape=outs,
        in_specs=ins,
        out_specs=places or [VMEM] * len(outs),
        scratch_shapes=list(scratch),
        cost_estimate=pl.CostEstimate(flops=int(cost * 1.15e9), bytes_accessed=1 << 20, transcendentals=0),
        compiler_params=pltpu.CompilerParams(vmem_limit_bytes=int(limit * 2**20)),
    )


def sds(shape, dtype):
    return jax.ShapeDtypeStruct(shape, dtype)


def lane_ids(rows):
    return lax.broadcasted_iota(jnp.int32, (rows, LANES), 1)


def split3(value):
    high = value.astype(BF16)
    rest = value - high.astype(F32)
    mid = rest.astype(BF16)
    low = (rest - mid.astype(F32)).astype(BF16)
    return high, mid, low


def pack_stats(stats):
    high, mid, low = (part.astype(F32) for part in split3(stats))
    return (high + pltpu.roll(mid, 8, 1) + pltpu.roll(low, 16, 1)).astype(BF16)


def unpack_stats(packed):
    packed = packed.astype(F32)
    return (packed + pltpu.roll(packed, LANES - 8, 1)) + pltpu.roll(packed, LANES - 16, 1)


def reorder(rows, source, x):
    shape = (rows, x.shape[0])
    row = lax.broadcasted_iota(jnp.int32, shape, 0)
    col = lax.broadcasted_iota(jnp.int32, shape, 1)
    pick = jnp.where(col == source(row), 1.0, 0.0).astype(BF16)
    return jnp.dot(pick, x, preferred_element_type=F32)


def project_kernel(
    steps,
    seq_ref,
    x_hbm,
    gain_hbm,
    wq_hbm,
    wk_hbm,
    wv_hbm,
    acc_ref,
    msg1_ref,
    msg2_ref,
    msg3_ref,
    x_ref,
    gain_ref,
    wq_ref,
    wk_ref,
    wv_ref,
    sems,
):
    copies = [
        pltpu.make_async_copy(source, target, sems.at[i])
        for i, (source, target) in enumerate(
            (
                (x_hbm, x_ref),
                (gain_hbm, gain_ref),
                (wq_hbm, wq_ref),
                (wk_hbm, wk_ref),
                (wv_hbm, wv_ref),
            )
        )
    ]
    for copy in copies:
        copy.start()
    copies[0].wait()
    copies[1].wait()
    rows = x_ref.shape[0]
    requests = rows // steps
    cut = requests // 4
    part = rows // 4
    place = seq_ref[0] & 3

    def source(row):
        return row % steps * requests + ((row // part) ^ place) * cut + row % part // steps

    x = reorder(rows, source, x_ref[...])
    normed = (x * gain_ref[...].astype(F32)).astype(BF16)
    squares = jnp.sum(x * x, axis=1, keepdims=True)
    msgs = (msg1_ref, msg2_ref, msg3_ref)
    at = 0
    for copy, w_ref in zip(copies[2:], (wq_ref, wk_ref, wv_ref)):
        copy.wait()
        width = w_ref.shape[1]
        product = jnp.dot(normed, w_ref[...], preferred_element_type=F32)
        acc_ref[:, at : at + width] = product[:part]
        for j, ref in enumerate(msgs):
            ref[:, at : at + width] = product[(j + 1) * part : (j + 2) * part].astype(BF16)
        at += width
    stats = jnp.where(lane_ids(rows) == 0, squares, 0.0)
    acc_ref[:, at:] = stats[:part]
    packed = pack_stats(stats)
    for j, ref in enumerate(msgs):
        ref[:, at:] = packed[(j + 1) * part : (j + 2) * part]


def keep_kernel(in_ref, out_ref):
    out_ref[...] = in_ref[...]


def add_kernel(acc_ref, *refs):
    *recv_refs, out_ref, msg_ref = refs
    at = acc_ref.shape[1] - LANES
    total, stats = acc_ref[:, :at], acc_ref[:, at:]
    for ref in recv_refs:
        total += ref[:, :at].astype(F32)
        stats += unpack_stats(ref[:, at:])
    stats = jnp.where(lane_ids(stats.shape[0]) == 0, stats, 0.0)
    out_ref[:, :at] = total
    msg_ref[:, :at] = total.astype(BF16)
    out_ref[:, at:] = stats
    msg_ref[:, at:] = pack_stats(stats)


def rotate_kernel(heads, kv, hd, features, acc_ref, recv_ref, cos_ref, sin_ref, out_ref):
    at = (heads + 2 * kv) * hd
    squares = acc_ref[:, at:] + unpack_stats(recv_ref[:, at:])
    scale = lax.rsqrt(squares[:, 0:1] / features + 1e-05)
    for index in range(heads + 2 * kv):
        cols = slice(index * hd, (index + 1) * hd)
        value = (acc_ref[:, cols] + recv_ref[:, cols].astype(F32)) * scale
        if index < heads + kv:
            value = value * cos_ref[...] + pltpu.roll(value, hd // 2, 1) * sin_ref[...]
        out_ref[:, cols] = value.astype(BF16)


def attend_kernel(heads, kv, steps, span, slots, seq_ref, len_ref, *refs):
    rows_refs, refs = refs[: len(slots)], refs[len(slots) :]
    k_ref, v_ref, *outs = refs[:-7]
    q_buf, kn_buf, vn_buf, s_buf, o_buf, m_buf, l_buf = refs[-7:]
    requests, rows_kv, hd = k_ref.shape
    cut = requests // 4
    part = cut * steps
    group = heads // kv
    block = steps * heads
    fresh = steps * kv
    seq = seq_ref[0]
    first = seq * span
    taken = [((seq & 3) ^ slot) * cut + r for slot in slots for r in range(cut)]

    for n, rows_ref in enumerate(rows_refs):

        def spread(buf, index, place, per_row):
            value = rows_ref[:, index * hd : (index + 1) * hd].astype(F32)
            buf[pl.ds(n * part * per_row + place, part, stride=per_row), :] = value

        for h in range(heads):
            spread(q_buf, h, h, heads)
        for g in range(kv):
            spread(kn_buf, heads + g, g, kv)
            spread(vn_buf, heads + kv + g, g, kv)
    shrink = hd ** (-0.5)
    queries = q_buf[...].astype(BF16)

    row = lax.broadcasted_iota(jnp.int32, (block, rows_kv), 0)
    col = lax.broadcasted_iota(jnp.int32, (block, rows_kv), 1)
    need = jnp.where((row % heads) // group == col % kv, col // kv, 1 << 29)
    for r, request in enumerate(taken):
        scores = lax.dot_general(
            queries[r * block : (r + 1) * block],
            k_ref[request],
            (((1,), (1,)), ((), ())),
            preferred_element_type=F32,
        )
        live = need < len_ref[request] - first
        s_buf[r * block : (r + 1) * block, :] = jnp.where(live, scores * shrink, -1e30)

    k_new = kn_buf[...].astype(BF16)
    v_new = vn_buf[...].astype(BF16)
    shape = (len(taken) * block, len(taken) * fresh)
    row = lax.broadcasted_iota(jnp.int32, shape, 0)
    col = lax.broadcasted_iota(jnp.int32, shape, 1)
    col_row = lax.broadcasted_iota(jnp.int32, (1, shape[1]), 1)
    at_position = (col_row % fresh) // kv - first
    for r, request in enumerate(taken):
        at_position += jnp.where(col_row // fresh == r, len_ref[request], 0)
    held = (at_position >= 0) & (at_position < span)
    new_live = (
        (row // block == col // fresh)
        & ((row % heads) // group == col % kv)
        & ((row % block) // heads >= (col % fresh) // kv)
        & held
    )
    new_scores = lax.dot_general(queries, k_new, (((1,), (1,)), ((), ())), preferred_element_type=F32)
    new_scores = jnp.where(new_live, new_scores * shrink, -1e30)

    scores = s_buf[...]
    top = jnp.maximum(jnp.max(scores, axis=1, keepdims=True), jnp.max(new_scores, axis=1, keepdims=True))
    top = jnp.maximum(top, -1e29)
    expo = jnp.exp(scores - top)
    new_expo = jnp.exp(new_scores - top)
    total = jnp.sum(expo, axis=1, keepdims=True) + jnp.sum(new_expo, axis=1, keepdims=True)
    m_buf[...] = jnp.broadcast_to(top, m_buf.shape)
    l_buf[...] = jnp.broadcast_to(total, l_buf.shape)
    expo = expo.astype(BF16)
    new_part = jnp.dot(new_expo.astype(BF16), v_new, preferred_element_type=F32)
    for r, request in enumerate(taken):
        mine = slice(r * block, (r + 1) * block)
        o_buf[mine, :] = new_part[mine] + jnp.dot(expo[mine], v_ref[request], preferred_element_type=F32)

    lane = lane_ids(part)
    for n, slot in enumerate(slots):
        stats = jnp.zeros((part, LANES), F32)
        for h in range(heads):
            take = pl.ds(n * part * heads + h, part, stride=heads)
            value = o_buf[take, :]
            cols = slice(h * hd, (h + 1) * hd)
            if slot:
                outs[n][:, cols] = value.astype(BF16)
            else:
                outs[0][:, cols] = value
            stats = jnp.where(lane == h, m_buf[take, :], stats)
            stats = jnp.where(lane == 24 + h, l_buf[take, :], stats)
        if slot:
            outs[n][:, heads * hd :] = pack_stats(stats)
        else:
            outs[1][...] = stats


def merged(heads, o_ref, st_ref, recv_refs):
    hd = o_ref.shape[1] // heads
    stats = [st_ref[...]] + [unpack_stats(ref[:, heads * hd :]) for ref in recv_refs]
    top = functools.reduce(jnp.maximum, stats)
    factors = [jnp.exp(one - top) for one in stats]
    total = sum(one * pltpu.roll(factor, 24, 1) for one, factor in zip(stats, factors))
    lane = lane_ids(top.shape[0])
    joint = jnp.where(lane < heads, top, jnp.where((lane >= 24) & (lane < 24 + heads), total, 0.0))

    def head(h):
        cols = slice(h * hd, (h + 1) * hd)
        value = o_ref[:, cols] * factors[0][:, h : h + 1]
        for ref, factor in zip(recv_refs, factors[1:]):
            value += ref[:, cols].astype(F32) * factor[:, h : h + 1]
        return value

    return joint, head


def merge_kernel(heads, o_ref, st_ref, *refs):
    *recv_refs, o_out, st_out, msg_out = refs
    stats, head = merged(heads, o_ref, st_ref, recv_refs)
    hd = o_ref.shape[1] // heads
    for h in range(heads):
        value = head(h)
        o_out[:, h * hd : (h + 1) * hd] = value
        msg_out[:, h * hd : (h + 1) * hd] = value.astype(BF16)
    st_out[...] = stats
    msg_out[:, heads * hd :] = pack_stats(stats)


def finish_kernel(heads, o_ref, st_ref, recv_ref, after_ref, att_ref, done_ref):
    stats, head = merged(heads, o_ref, st_ref, [recv_ref])
    done_ref[...] = after_ref[...]
    hd = o_ref.shape[1] // heads
    for h in range(heads):
        att_ref[:, h * hd : (h + 1) * hd] = (head(h) / stats[:, 24 + h : 25 + h]).astype(BF16)


def store_kernel(column, steps, span, seq_ref, len_ref, *refs):
    slot_refs, (c_ref, after_ref, c_out, done_ref, buf, win, sems) = refs[:4], refs[4:]
    done_ref[...] = after_ref[...]
    requests, rows_kv, hd = c_ref.shape
    window = win.shape[1]
    kv = rows_kv // span
    cut = requests // 4
    fresh = steps * kv
    seq = seq_ref[0]
    whole = pltpu.make_async_copy(c_ref, c_out, sems.at[requests])
    whole.start()
    for g in range(kv):
        at = column + g * hd
        for j, ref in enumerate(slot_refs):
            buf[pl.ds(j * cut * fresh + g, cut * steps, stride=kv), :] = ref[:, at : at + hd].astype(F32)
    line = lax.broadcasted_iota(jnp.int32, (window, hd), 0)
    place = lax.broadcasted_iota(jnp.int32, (window, fresh), 0) - lax.broadcasted_iota(
        jnp.int32, (window, fresh), 1
    )
    pieces = []
    for n in range(requests):
        request = ((seq & 3) ^ (n // cut)) * cut + n % cut
        base = (len_ref[request] - seq * span) * kv
        start = pl.multiple_of(jnp.clip((base // 16) * 16, 0, rows_kv - window), 16)
        touched = (base > -fresh) & (base < rows_kv)
        pieces.append((touched, start, request))

        @pl.when(touched)
        def _():
            pick = jnp.where(place == base - start, 1.0, 0.0).astype(BF16)
            new = (line >= base - start) & (line < base - start + fresh)
            rows = buf[n * fresh : (n + 1) * fresh, :].astype(BF16)
            put = jnp.dot(pick, rows, preferred_element_type=F32)
            old = c_ref[request, pl.ds(start, window), :].astype(F32)
            win[n] = jnp.where(new, put, old).astype(BF16)

    whole.wait()
    for act in ("start", "wait"):
        for n, (touched, start, request) in enumerate(pieces):

            @pl.when(touched)
            def _():
                copy = pltpu.make_async_copy(win.at[n], c_out.at[request, pl.ds(start, window), :], sems.at[n])
                getattr(copy, act)()


def mix_kernel(seq_ref, core_ref, a0_ref, a1_ref, a2_ref, a3_ref, w_ref, done_ref, mine_ref, other_ref, att_buf):
    part = a0_ref.shape[0]
    for j, ref in enumerate((a0_ref, a1_ref, a2_ref, a3_ref)):
        att_buf[pl.ds(pl.multiple_of(((seq_ref[0] & 3) ^ j) * part, 16), part), :] = ref[...]
    product = jnp.dot(att_buf[...], w_ref[...], preferred_element_type=F32)
    half = product.shape[0] // 2
    low = core_ref[0] == 0
    mine_ref[...] = jnp.where(low, product[:half], product[half:])
    other_ref[...] = jnp.where(low, product[half:], product[:half])


def stack_kernel(*refs):
    *in_refs, out_ref = refs
    at = 0
    for ref in in_refs:
        out_ref[at : at + ref.shape[0]] = ref[...]
        at += ref.shape[0]


def relay_kernel(in_ref, after_ref, out_ref):
    del after_ref
    out_ref[...] = in_ref[...]


def sum_kernel(mine_ref, recv_ref, *msg_refs):
    count = mine_ref.shape[0] // len(msg_refs)
    for i, ref in enumerate(msg_refs):
        some = slice(i * count, (i + 1) * count)
        ref[...] = (mine_ref[some].astype(F32) + recv_ref[some].astype(F32)).astype(BF16)


def residual_kernel(steps, core_ref, x_ref, gain_ref, mine_ref, recv_ref, mixed_ref, piece_ref):
    rows = mine_ref.shape[0]
    requests = x_ref.shape[0] // steps
    cut = requests // 4
    core = core_ref[0]

    def source(row):
        quarter = row // (rows // 2)
        request = quarter * cut + row % (rows // 2) // steps
        return row % steps * requests + core * (requests // 2) + request

    part = mine_ref[...].astype(F32) + recv_ref[...].astype(F32)
    mixed = reorder(rows, source, x_ref[...]) + part
    mixed_ref[...] = mixed
    squares = jnp.sum(mixed * mixed, axis=1, keepdims=True)
    stats = jnp.where(lane_ids(rows) == 0, squares, 0.0)
    piece_ref[0, :, :LANES] = pack_stats(stats)
    piece_ref[0, :, LANES:] = (mixed * gain_ref[...].astype(F32)).astype(BF16)


def gather_products(masks, seq, own_ref, far_ref, wg_ref, wu_ref, so_far):
    width = own_ref.shape[2] - LANES
    squares = []
    for ref in (own_ref, far_ref):
        squares.append(sum(unpack_stats(ref[j, :, :LANES]) for j in range(len(masks))))
    squares = jnp.concatenate(squares, axis=0)
    gate = up = 0.0
    for j, mask in enumerate(masks):
        take = pl.ds(pl.multiple_of((seq ^ mask) * width, 16), width)
        x = jnp.concatenate([own_ref[j, :, LANES:], far_ref[j, :, LANES:]], axis=0)
        gate += jnp.dot(x, wg_ref[take, :], preferred_element_type=F32)
        up += jnp.dot(x, wu_ref[take, :], preferred_element_type=F32)
    return [new + ref[...] for new, ref in zip((squares, gate, up), so_far)] if so_far else (squares, gate, up)


def products_kernel(masks, features, taken, seq_ref, own_ref, far_ref, wg_ref, wu_ref, *refs):
    copies = []
    if taken:
        w_hbm, *refs = refs
        refs, w_refs, sems = refs[: -len(taken) - 1], refs[-len(taken) - 1 : -1], refs[-1]
        for i, (some, w_ref) in enumerate(zip(taken, w_refs)):
            width = w_ref.shape[2]
            for j, mask in enumerate(some):
                at = pl.multiple_of((seq_ref[0] ^ mask) * width, LANES)
                copies.append(pltpu.make_async_copy(w_hbm.at[:, pl.ds(at, width)], w_ref.at[j], sems.at[i, j]))
                copies[-1].start()
    outs = refs[-1:] if features else refs[-3:]
    found = gather_products(masks, seq_ref[0], own_ref, far_ref, wg_ref, wu_ref, refs[: -len(outs)])
    if features:
        found = [hidden_units(features, *found)]
    for ref, value in zip(outs, found):
        ref[...] = value
    for copy in copies:
        copy.wait()


def hidden_units(features, squares, gate, up):
    scale = lax.rsqrt(squares[:, 0:1] / features + 1e-05)
    gate = gate * scale
    up = up * scale
    return (gate / (1.0 + jnp.exp(-gate)) * up).astype(BF16)


def down_kernel(count, h_ref, *refs):
    own_ref, far_ref = refs[-2:]
    half = own_ref.shape[1]
    hidden = h_ref[...]
    at = 0
    for w_ref in refs[:count]:
        for j in range(w_ref.shape[0]):
            part = jnp.dot(hidden, w_ref[j], preferred_element_type=F32)
            own_ref[at + j] = part[:half]
            far_ref[at + j] = part[half:].astype(BF16)
        at += w_ref.shape[0]


def fold_kernel(acc_ref, *refs):
    *recv_refs, keep_ref, msg_ref = refs
    count = acc_ref.shape[0] // 2
    for j in range(2 * count):
        total = acc_ref[j]
        for ref in recv_refs:
            total += ref[j].astype(F32)
        if j < count:
            keep_ref[j] = total
        else:
            msg_ref[j - count] = total.astype(BF16)


def end_kernel(mixed_ref, mine_ref, recv_ref, out_ref):
    part = mine_ref[0].astype(F32) + recv_ref[0].astype(F32)
    out_ref[...] = (mixed_ref[...] + part).astype(BF16)


def join_kernel(steps, core_ref, own_ref, far_ref, out_ref):
    rows = out_ref.shape[0]
    requests = rows // steps
    cut = requests // 4
    low = core_ref[0] == 0
    own, far = own_ref[...], far_ref[...]
    whole = jnp.concatenate([jnp.where(low, own, far), jnp.where(low, far, own)], axis=0)

    def source(row):
        request = row % requests
        return request * steps + row // requests

    out_ref[...] = reorder(rows, source, whole).astype(BF16)


def per_device(
    n_seq,
    n_tp,
    tokens,
    attn_gain,
    w_query,
    w_key,
    w_value,
    w_out,
    ffn_gain,
    w_gate,
    w_up,
    w_down,
    key_cache,
    value_cache,
    lengths,
):
    steps, requests, width = tokens.shape
    span, kv, hd = key_cache.shape[1:]
    heads = w_query.shape[1] // hd
    cut = requests // 4
    part = steps * cut
    half, rows = 2 * part, 4 * part
    features = width * n_seq
    hidden_width = w_gate.shape[1]
    wide = w_query.shape[1] + w_key.shape[1] + w_value.shape[1] + LANES
    seq = lax.axis_index("seq").astype(jnp.int32)
    core = lax.axis_index("tp").astype(jnp.int32) & 1
    seq_arr, core_arr = seq.reshape(1), core.reshape(1)
    rest = [1 << b for b in range(2, n_seq.bit_length() - 1)]
    tp_bits = [1 << b for b in range(n_tp.bit_length() - 1)]
    masks = [0]
    for bit in reversed(rest):
        masks = masks + [m ^ bit for m in masks]
    slots = [[m ^ j for m in masks] for j in range(4)]

    def hop(value, axis, bit):
        size = n_seq if axis == "seq" else n_tp
        return lax.ppermute(value, axis, [(i, i ^ bit) for i in range(size)])

    x = tokens.reshape(rows, width)
    flat = (requests, span * kv, hd)
    k_flat, v_flat = key_cache.reshape(flat), value_cache.reshape(flat)

    own_lengths = lax.dynamic_slice_in_dim(lengths, (seq & 3) * cut, cut, 0)
    positions = (own_lengths[:, None] + jnp.arange(steps, dtype=jnp.int32)[None, :]).reshape(part)
    freqs = jnp.exp(jnp.arange(hd // 2, dtype=F32) * (-2.0 * math.log(100000000.0) / hd))
    angles = positions.astype(F32)[:, None] * freqs[None, :]
    cosine, sine = jnp.cos(angles), jnp.sin(angles)
    cosine = jnp.concatenate([cosine, cosine], axis=1)
    sine = jnp.concatenate([-sine, sine], axis=1)

    with jax.named_scope("project"):
        sums = [sds((part, wide), F32), sds((part, wide), BF16)]
        acc, *msgs = call(
            functools.partial(project_kernel, steps),
            sums + sums[1:] * 2,
            [SMEM] + [HBM] * 5,
            [
                pltpu.VMEM(x.shape, BF16),
                pltpu.VMEM(attn_gain.shape, BF16),
                pltpu.VMEM(w_query.shape, BF16),
                pltpu.VMEM(w_key.shape, BF16),
                pltpu.VMEM(w_value.shape, BF16),
                pltpu.SemaphoreType.DMA((5,)),
            ],
            limit=60,
        )(seq_arr, x, attn_gain, w_query, w_key, w_value)
        arrived = [hop(msgs[j - 1], "seq", j) for j in (3, 2, 1)]
        (acc,) = call(keep_kernel, sums[:1], [VMEM])(acc)
        for bit in rest:
            acc, msg = call(add_kernel, sums, [VMEM] * (1 + len(arrived)))(acc, *arrived)
            arrived = [hop(msg, "seq", bit)]
        (finished,) = call(
            functools.partial(rotate_kernel, heads, kv, hd, features),
            [sds((part, wide - LANES), BF16)],
            [VMEM] * 4,
        )(acc, arrived[0], cosine, sine)
        found = {j: hop(finished, "seq", j) for j in (3, 2, 1)}
        found[0] = finished

    with jax.named_scope("attend"):
        block = steps * heads
        fresh = steps * kv
        joint = [
            sds((part, heads * hd), F32),
            sds((part, LANES), F32),
            sds((part, heads * hd + LANES), BF16),
        ]
        def attend(*some):
            count = len(some) * cut
            return call(
                functools.partial(attend_kernel, heads, kv, steps, span, some),
                joint[2:] * len(some) if some[0] else joint[:2],
                [SMEM, SMEM] + [VMEM] * (len(some) + 2),
                [
                    pltpu.VMEM((count * block, hd), F32),
                    pltpu.VMEM((count * fresh, hd), F32),
                    pltpu.VMEM((count * fresh, hd), F32),
                    pltpu.VMEM((count * block, flat[1]), F32),
                    pltpu.VMEM((count * block, hd), F32),
                    pltpu.VMEM((count * block, hd), F32),
                    pltpu.VMEM((count * block, hd), F32),
                ],
                cost=20,
            )(seq_arr, lengths, *(found[j] for j in some), k_flat, v_flat)

        o, st = attend(0)
        arrived = [hop(msg, "seq", j) for some in ((3,), (1, 2)) for j, msg in zip(some, attend(*some))]
        for bit in rest:
            o, st, msg = call(
                functools.partial(merge_kernel, heads), joint, [VMEM] * (2 + len(arrived))
            )(o, st, *arrived)
            arrived = [hop(msg, "seq", bit)]

        def store(column, cache, after):
            return call(
                functools.partial(store_kernel, column * hd, steps, span),
                [sds(flat, BF16), sds((part, LANES), F32)],
                [SMEM, SMEM] + [VMEM] * 6,
                [
                    pltpu.VMEM((requests * fresh, hd), F32),
                    pltpu.VMEM((requests, 16 + -(-fresh // 16) * 16, hd), BF16),
                    pltpu.SemaphoreType.DMA((requests + 1,)),
                ],
                [HBM, VMEM],
            )(seq_arr, lengths, *(found[j] for j in range(4)), cache, after)

        keys, done = store(heads, k_flat, st)
        attended, done = call(
            functools.partial(finish_kernel, heads),
            [sds((part, heads * hd), BF16), sds((part, LANES), F32)],
            [VMEM] * 4,
        )(o, st, arrived[0], done)
        values, done = store(heads + kv, v_flat, done)
        found = {j: hop(attended, "seq", j) for j in (3, 2, 1)}
        found[0] = attended

    with jax.named_scope("mix"):
        mine, other = call(
            mix_kernel,
            [sds((half, width), F32)] * 2,
            [SMEM, SMEM] + [VMEM] * 6,
            [pltpu.VMEM((rows, heads * hd), BF16)],
        )(seq_arr, core_arr, *(found[j] for j in range(4)), w_out, done)
        summed = mine, hop(other, "tp", 1)
        for bit in tp_bits[1:]:
            (msg,) = call(sum_kernel, [sds((half, width), BF16)], [VMEM] * 2)(*summed)
            summed = msg, hop(msg, "tp", bit)
        gain = lax.dynamic_slice_in_dim(ffn_gain, seq * width, width, 0).reshape(1, width)
        mixed, pieces = call(
            functools.partial(residual_kernel, steps),
            [sds((half, width), F32), sds((1, half, LANES + width), BF16)],
            [SMEM] + [VMEM] * 4,
            cost=6,
        )(core_arr, x, gain, *summed)
        for bit in reversed(rest):
            (pieces,) = call(
                stack_kernel,
                [sds((2 * pieces.shape[0],) + pieces.shape[1:], BF16)],
                [VMEM] * 2,
                cost=8,
            )(pieces, hop(pieces, "seq", bit))

    with jax.named_scope("ffn"):
        found = {j: hop(pieces, "seq", j) for j in (3, 2, 1)}
        found[0] = pieces
        order = (0, 2, 1, 3)
        reads = ((3,), (2,), (1,), (0,))
        state = []
        earlier = []
        quarter = {}
        for n, j in enumerate(order):
            piece = found[j]
            if n:
                (piece,) = call(relay_kernel, [sds(piece.shape, BF16)], [VMEM] * 2, cost=1)(
                    piece, earlier[max(n - 2, 0)]
                )
            taken = reads[n] if width % LANES == 0 else ()
            state = call(
                functools.partial(
                    products_kernel, slots[j], features if n == 3 else 0, [slots[i] for i in taken]
                ),
                (
                    [sds((rows, hidden_width), BF16)]
                    if n == 3
                    else [sds((rows, LANES), F32)] + [sds((rows, hidden_width), F32)] * 2
                )
                + [sds((len(masks), hidden_width, width), BF16)] * len(taken),
                [SMEM] + [VMEM] * 4 + [HBM] * (len(taken) > 0) + [VMEM] * len(state),
                [pltpu.SemaphoreType.DMA((len(taken), len(masks)))] * (len(taken) > 0),
                cost=1,
            )(seq_arr, found[j], hop(piece, "tp", 1), w_gate, w_up, *[w_down] * (len(taken) > 0), *state)
            if taken:
                quarter.update(zip(taken, state[-len(taken) :]))
                state = state[: -len(taken)]
            earlier.append(state[0])
        (hidden,) = state

        def down(some, *after):
            shape = (len(some) * len(masks), half, width)
            if quarter:
                return call(
                    functools.partial(down_kernel, len(some)),
                    [sds(shape, F32), sds(shape, BF16)],
                    [VMEM] * (1 + len(some) + len(after)),
                    cost=1,
                )(hidden, *(quarter[j] for j in some), *after)
            whole = jnp.dot(hidden, w_down, preferred_element_type=F32)
            whole = whole.reshape(rows, n_seq, width).transpose(1, 0, 2)
            places = [m for j in some for m in slots[j]]
            whole = jnp.take(whole, seq ^ jnp.array(places, jnp.int32), axis=0)
            return whole[:, :half], whole[:, half:].astype(BF16)

        shape = (len(masks), half, width)
        arrived = []
        sent = []
        after = []
        for some in ((3,), (1, 2)):
            own, far = down(some, *after)
            after = [far]
            msgs = call(sum_kernel, [sds(shape, BF16)] * len(some), [VMEM] * 2)(own, hop(far, "tp", 1))
            sent += msgs
            arrived += [hop(msg, "seq", j) for j, msg in zip(some, msgs)]
        keep, far = down((0,), *sent)
        arrived.append(hop(far, "tp", 1))
        for bit in rest:
            shape = (keep.shape[0] // 2, half, width)
            keep, msg = call(fold_kernel, [sds(shape, F32), sds(shape, BF16)], [VMEM] * (1 + len(arrived)))(
                keep, *arrived
            )
            arrived = [hop(msg, "seq", bit)]
        shape = (1, half, width)
        summed = keep, arrived[0]
        for bit in tp_bits[1:]:
            (msg,) = call(sum_kernel, [sds(shape, BF16)], [VMEM] * 2)(*summed)
            summed = msg, hop(msg, "tp", bit)
        (own,) = call(end_kernel, [sds((half, width), BF16)], [VMEM] * 3)(mixed, *summed)
        (result,) = call(functools.partial(join_kernel, steps), [sds(x.shape, BF16)], [SMEM] + [VMEM] * 2)(
            core_arr, own, hop(own, "tp", 1)
        )
    return result.reshape(tokens.shape), keys.reshape(key_cache.shape), values.reshape(value_cache.shape)


def solution(mesh):
    placed = (
        P(None, None, "seq"),
        P("seq"),
        P("seq", "tp"),
        P("seq", "tp"),
        P("seq", "tp"),
        P("tp", "seq"),
        P(),
        P(None, ("seq", "tp")),
        P(None, ("seq", "tp")),
        P(("seq", "tp"), None),
        P(None, "seq", "tp", None),
        P(None, "seq", "tp", None),
        P(),
    )
    return jax.shard_map(
        functools.partial(per_device, mesh.shape["seq"], mesh.shape["tp"]),
        mesh=mesh,
        in_specs=placed,
        out_specs=(P(None, None, "seq"), P(None, "seq", "tp", None), P(None, "seq", "tp", None)),
        check_vma=False,
    )
```
